128 devices in a mesh: col: 8 (over z, core), row: 16 (over x, y).
Axes of the slice: x: 4, y: 4, z: 4, core: 2. Of those that a mesh axis runs over, the one named last changes fastest.
Arguments:
- block_pixels: float32 [16384, 8, 256], P(('col', 'row')), may hold values from -6 to 6
- block_ivar: bfloat16 [16384, 8, 256], P(('col', 'row')), may hold values from 0.29882812 to 3
- block_mask: int32 [16384, 8, 256], P(('col', 'row')), may hold values 0 or 1
- block_patch: int32 [16384, 1], P(('col', 'row')), may hold values from 0 to 127; in each aligned block of 128 rows (0 to 127, 128 to 255, ...) at most 2 rows name the same one
- block_offset: int32 [16384], P(('col', 'row')), may hold values from 0 to 120
- block_exposure: int32 [16384], P(('col', 'row')), may hold values from 0 to 95
- exposure_band: int32 [96], replicated, may hold values from 0 to 5
- basis: float32 [5, 41, 41], replicated, may hold values from -0.15625 to 0.15625
- coefficients: float32 [16, 8, 6, 5], P('row', 'col'), may hold values from -3 to 3
Outputs:
- coadd: float32 [6, 2048, 2048], P(None, 'row', 'col')
The draws below stay inside these ranges and needn't reach their ends.
Inputs may be any that keep to these rules, and one draw needn't show every extreme that they name: `block_patch`: among the blocks of one device at most 2 name the same patch, a bound that some block reaches.
All inputs are finite; a program needn't handle non-finite values. No bound on the sum of `block_mask` on one device may be relied on, other than what follows from the above.
Results may differ from the reference program's by a relative error of at most 0.0049.
Values may be sent and summed in bfloat16 or wider, within the bound.
A program may use at most 64 MiB of HBM per device.

```python
import math
import jax
import jax.numpy as jnp
import numpy as np
from jax import lax

BANDS = 6
NBASIS = 5
KS = 41
HALF = 20
EXPOSURES = 96
PH = 128
PW = 256
BH = 8
NB_DEV = 128
CAP = 2
NBLK = 16384
PATCH_ROWS = 16
PATCH_COLS = 8
N_COL = 8
N_ROW = 16
DEVICES = 128


def with_ends(values, rng, low, top_value):
    extent = values.shape
    place = [jax.random.randint(jax.random.fold_in(rng, axis), (), 0, extent[axis]) for axis in range(len(extent))]
    values = values.at[tuple(place)].set(low)
    longest = extent.index(max(extent))
    place[longest] = (place[longest] + 1) % extent[longest]
    return values.at[tuple(place)].set(top_value)


def shard_levels(own_key, shape, shards, low, largest):
    def one(axis_at, parts):
        steps = jax.random.uniform(jax.random.fold_in(jax.random.fold_in(own_key, 6), axis_at), (parts,), jnp.float32, low / len(shards), largest / len(shards))
        return jnp.repeat(jnp.exp(steps), shape[axis_at] // parts).reshape((-1,) + (1,) * (len(shape) - axis_at - 1))

    loudness = one(*shards[0])
    for cut in shards[1:]:
        loudness = loudness * one(*cut)
    return loudness


def assign_block(stream_key, own, number, rows, number_of, top, most, skew):
    sequence = jax.random.permutation(stream_key, number_of)
    packed, usual = portions_of(number_of, rows * top, most, skew, True), portions_of(number_of, rows * top, most, skew, False)
    places = jnp.arange(number_of)

    def named(lengths, offset_by):
        used = int((lengths > 0).sum())
        fixed = max(1, used // 4)
        passed = fixed + (places - fixed + offset_by * (used - fixed)) % max(1, number_of - fixed)
        return jnp.zeros((number_of,), jnp.int32).at[sequence[jnp.where(places < fixed, places, passed)]].set(jnp.asarray(lengths, jnp.int32))

    lengths = jnp.where(number % 4 == 0, named(packed, number // 4), named(usual, number - number // 4 - 1))
    mixed = jax.random.permutation(jax.random.fold_in(own, 3), number_of)
    giver, receiver = mixed[0:number_of // 2 * 2:2], mixed[1:number_of // 2 * 2:2]
    room = jnp.minimum(lengths[giver] - 1, most - lengths[receiver]) // 2
    room = jnp.where((giver == sequence[0]) | (receiver == sequence[0]) | (lengths[receiver] == 0), 0, jnp.maximum(room, 0))
    passed = jax.random.randint(jax.random.fold_in(own, 4), (number_of // 2,), 0, 1 << 20) % (room + 1)
    lengths = lengths.at[giver].add(-passed).at[receiver].add(passed)
    members = jnp.searchsorted(jnp.cumsum(lengths), jnp.arange(rows * top), side="right").astype(jnp.int32)
    table = members.reshape(top, rows).T
    table = table[jax.random.permutation(jax.random.fold_in(own, 1), rows)]
    offset_by = jax.random.randint(jax.random.fold_in(own, 2), (rows, 1), 0, top)
    return jnp.take_along_axis(table, (jnp.arange(top)[None, :] + offset_by) % top, axis=1)


def portions_of(amount, total, limit, lean, full):
    loads = [(1 << 20) // math.isqrt(rank ** lean) + 1 for rank in range(1, amount + 1)]
    largest = limit if full else min(limit, max(-(-total // amount), total * loads[0] // sum(loads)))
    least = 1 if total - largest >= amount - 1 else 0
    counts, rest = [largest] + [least] * (amount - 1), total - largest - least * (amount - 1)
    while rest > 0:
        free = [i for i in range(1, amount) if counts[i] < largest] or [i for i in range(1, amount) if counts[i] < limit]
        pool, remaining = sum([loads[i] for i in free]), rest
        for i in free:
            more = min(limit - counts[i], max(1, remaining * loads[i] // pool), rest)
            counts[i] = counts[i] + more
            rest = rest - more
    return np.array(counts)


def bell_draw(stream_key, dims, deviation, reach, cuts=(), held_as=jnp.bfloat16):
    array = deviation * jax.random.normal(stream_key, dims, jnp.float32)
    if cuts:
        array = array * shard_levels(stream_key, dims, cuts, -0.22, 0.18)
    return jnp.clip(array, -reach, reach).astype(held_as)


def setup_inputs(seed: int = 0) -> dict:
    splits = jax.random.split(jax.random.key(seed), 10)
    block_pixels = bell_draw(splits[0], (NBLK, BH, PW), 1.0, 6.0, ((0, 128),), jnp.float32)
    block_ivar = jnp.clip(jnp.exp(math.log(3.0) - 2.306499 * jax.random.uniform(splits[1], (NBLK, BH, PW), jnp.float32) ** shard_levels(splits[1], (NBLK, BH, PW), ((0, 128),), -0.2, 0.2)), 0.29882812, 3.0).astype(jnp.bfloat16)
    block_mask = with_ends((jax.random.randint(splits[2], (NBLK, BH, PW), 0, 8) < 7).astype(jnp.int32), jax.random.fold_in(splits[2], 1), 0, 1)
    block_patch_keys = jax.random.split(jax.random.fold_in(splits[3], 1), NBLK // NB_DEV)
    block_patch_turns = jax.random.permutation(jax.random.fold_in(splits[3], 3), NBLK // NB_DEV)
    block_patch = jax.vmap(lambda own, number: assign_block(jax.random.fold_in(splits[3], 2), own, number, NB_DEV, DEVICES, 1, CAP, 2))(block_patch_keys, block_patch_turns).reshape((NBLK, 1))
    block_offset = with_ends(jax.random.randint(splits[4], (NBLK,), 0, PH - BH + 1), jax.random.fold_in(splits[4], 1), 0, PH - BH).astype(jnp.int32)
    block_exposure = with_ends(jax.random.randint(splits[5], (NBLK,), 0, EXPOSURES), jax.random.fold_in(splits[5], 1), 0, EXPOSURES - 1).astype(jnp.int32)
    exposure_band = with_ends(jax.random.randint(splits[6], (EXPOSURES,), 0, BANDS), jax.random.fold_in(splits[6], 1), 0, BANDS - 1).astype(jnp.int32)
    basis = bell_draw(splits[7], (NBASIS, KS, KS), (KS * KS) ** -0.5, 0.15625, (), jnp.float32)
    coefficients = bell_draw(splits[8], (PATCH_ROWS, PATCH_COLS, BANDS, NBASIS), 0.6, 3.0, ((0, 16), (1, 8)), jnp.float32)
    return dict(block_pixels=block_pixels, block_ivar=block_ivar, block_mask=block_mask, block_patch=block_patch, block_offset=block_offset, block_exposure=block_exposure, exposure_band=exposure_band, basis=basis, coefficients=coefficients)


def reference(block_pixels, block_ivar, block_mask, block_patch, block_offset, block_exposure, exposure_band, basis, coefficients):
    weight = block_mask.astype(jnp.float32) * block_ivar.astype(jnp.float32)
    weighted = (weight * block_pixels).astype(jnp.bfloat16)
    weight_low = weight.astype(jnp.bfloat16)
    target = block_patch[:, 0]
    patch_row = target % N_ROW
    patch_col = target // N_ROW
    band_ids = exposure_band[block_exposure]
    row_ids = band_ids[:, None] * (N_ROW * PH) + patch_row[:, None] * PH + block_offset[:, None] + jnp.arange(BH, dtype=jnp.int32)[None, :]
    segment_ids = (row_ids * N_COL + patch_col[:, None]).reshape(-1)
    payload = jnp.stack([weighted, weight_low], axis=2).astype(jnp.float32).reshape(NBLK * BH, 2, PW)
    sums = jax.ops.segment_sum(payload, segment_ids, num_segments=BANDS * N_ROW * PH * N_COL)
    sums = sums.reshape(BANDS, N_ROW * PH, N_COL, 2, PW)
    numerator = sums[:, :, :, 0, :].reshape(BANDS, N_ROW * PH, N_COL * PW)
    coverage = sums[:, :, :, 1, :].reshape(BANDS, N_ROW * PH, N_COL * PW)
    mean_image = (numerator / jnp.maximum(coverage, 1.0)).astype(jnp.bfloat16)
    padded = jnp.pad(mean_image.astype(jnp.float32), ((0, 0), (HALF, HALF), (HALF, HALF)))
    kernels = jnp.einsum('rcbk,kij->rcbij', coefficients.astype(jnp.float32), basis.astype(jnp.float32), precision=lax.Precision.HIGHEST).astype(jnp.bfloat16)

    def one_patch(patch_index):
        this_row = patch_index % N_ROW
        this_col = patch_index // N_ROW
        window = lax.dynamic_slice(padded, (jnp.int32(0), (this_row * PH).astype(jnp.int32), (this_col * PW).astype(jnp.int32)), (BANDS, PH + 2 * HALF, PW + 2 * HALF))
        kernel = kernels[this_row, this_col].astype(jnp.float32)
        result = lax.conv_general_dilated(window[None], kernel[:, None], (1, 1), 'VALID', feature_group_count=BANDS, precision=lax.Precision.HIGHEST)
        return result[0]

    patches = lax.map(one_patch, jnp.arange(N_COL * N_ROW, dtype=jnp.int32))
    patches = patches.reshape(N_COL, N_ROW, BANDS, PH, PW)
    return jnp.transpose(patches, (2, 1, 3, 0, 4)).reshape(BANDS, N_ROW * PH, N_COL * PW)
```

```python
import jax
import jax.numpy as jnp
from jax import lax
from jax.experimental import pallas as pl
from jax.experimental.pallas import tpu as pltpu
from jax.sharding import PartitionSpec as P

BANDS = 6
NBASIS = 5
KS = 41
HALF = 20
PH = 128
PW = 256
BH = 8
MESH = pl.DeviceIdType.MESH

STEP_X = (-1782682714, -1921033681, 1934304481, 809635604)
STEP_Y = (1734851178, 1843253947, 483576120, 202408901)
STEP_Z = (1524231834, 502626494, -985886066, 50605265)

GROUP = 4
TILE = 64
TAPS = 48
SHIFTS = TAPS // GROUP
ROWS = PH + 64
FIRST = 32 - HALF
OUT_ROWS = 528


def iota(shape, dim):
    return lax.broadcasted_iota(jnp.int32, shape, dim)


def body(
    coef_ref,
    patch_ref,
    offset_ref,
    exposure_ref,
    band_ref,
    basis_ref,
    pix_hbm,
    ivar_hbm,
    mask_hbm,
    out_hbm,
    pix,
    ivar,
    mask,
    table,
    table_s,
    label,
    label_in,
    data,
    data_in,
    sums,
    weights,
    mean_b,
    packs,
    above,
    below,
    side_l,
    side_r,
    image32,
    image2,
    prod,
    out_v,
    in_sem,
    table_sem,
    data_send,
    data_recv,
    label_send,
    label_recv,
    halo_send,
    halo_recv,
    out_sem,
):
    col = lax.axis_index("col")
    row = lax.axis_index("row")
    me = col * 16 + row
    z, core, x, y = col >> 1, col & 1, row >> 2, row & 3

    loads = [
        pltpu.make_async_copy(src, dst, in_sem.at[i])
        for i, (src, dst) in enumerate(((pix_hbm, pix), (ivar_hbm, ivar), (mask_hbm, mask)))
    ]
    barrier = pltpu.get_barrier_semaphore()

    def greet(k, _):
        peer = (me + k) & 127
        pl.semaphore_signal(barrier, inc=1, device_id=(peer >> 4, peer & 15), device_id_type=MESH)
        return 0

    lax.fori_loop(1, 128, greet, 0)
    for load in loads:
        load.start()

    square = (128, 128)
    sub, lane = iota(square, 0), iota(square, 1)
    diag = sub == lane

    def to_column(line):
        return jnp.sum(jnp.where(diag, line, 0.0), axis=1, keepdims=True)

    def to_line(column):
        return jnp.sum(jnp.where(diag, column, 0.0), axis=0, keepdims=True)

    subf, lanef = sub.astype(jnp.float32), lane.astype(jnp.float32)
    patch = patch_ref[...].astype(jnp.float32)
    band_col = to_column(band_ref[...].astype(jnp.float32))
    band_line = jnp.sum(
        jnp.where(exposure_ref[...].astype(jnp.float32) == subf, band_col, 0.0), axis=0, keepdims=True
    )
    key_line = band_line * float(PH) + offset_ref[...].astype(jnp.float32)
    named = patch == subf
    low = jnp.min(jnp.where(named, lanef, 128.0), axis=1, keepdims=True)
    high = jnp.max(jnp.where(named, lanef, -1.0), axis=1, keepdims=True)
    key_low = jnp.sum(jnp.where(lanef == low, key_line, 0.0), axis=1, keepdims=True)
    key_high = jnp.sum(jnp.where(lanef == high, key_line, 0.0), axis=1, keepdims=True)
    key_low = jnp.where(low < 128.0, key_low, -1000.0)
    key_high = jnp.where(high > low, key_high, -1000.0)
    place = (lane & 15) < BH
    label[...] = (jnp.where(place, key_low, key_high) + (lane & 7).astype(jnp.float32)).astype(jnp.int32)
    low_line = to_line(jnp.minimum(low, 127.0))
    high_line = to_line(jnp.maximum(high, 0.0))
    table[...] = jnp.where(iota((8, 128), 0) == 0, low_line, high_line).astype(jnp.int32)
    to_smem = pltpu.make_async_copy(table, table_s, table_sem)
    to_smem.start()
    to_smem.wait()

    for load in loads:
        load.wait()
    pl.semaphore_wait(barrier, 127)

    def fill(owner, into, at):
        first, second = table_s[0, owner] & 127, table_s[1, owner] & 127
        w0 = mask[first].astype(jnp.float32) * ivar[first].astype(jnp.float32)
        w1 = mask[second].astype(jnp.float32) * ivar[second].astype(jnp.float32)
        p0, p1 = w0 * pix[first], w1 * pix[second]
        into[pl.ds(at, 16), 0:PW] = jnp.concatenate([p0, p1], axis=0).astype(jnp.bfloat16)
        into[pl.ds(at, 16), PW : 2 * PW] = jnp.concatenate([w0, w1], axis=0).astype(jnp.bfloat16)

    def transfer(k, owner, group, target):
        rows = pl.ds(pl.multiple_of(k * 16, 16), 16)
        return (
            pltpu.make_async_remote_copy(
                src_ref=data.at[rows],
                dst_ref=data_in.at[rows],
                send_sem=data_send,
                recv_sem=data_recv.at[group],
                device_id=target,
                device_id_type=MESH,
            ),
            pltpu.make_async_remote_copy(
                src_ref=label.at[pl.ds(owner, 1)],
                dst_ref=label_in.at[pl.ds(k, 1)],
                send_sem=label_send,
                recv_sem=label_recv.at[group],
                device_id=target,
                device_id_type=MESH,
            ),
        )

    for group in range(8):
        words = [steps[group >> 1] for steps in (STEP_X, STEP_Y, STEP_Z)]

        def send(m, _, group=group, words=words):
            k = group * 16 + m
            shift = ((group & 1) * 8 + (m >> 1)) * 2
            dx, dy, dz = [(jnp.int32(word) >> shift) & 3 for word in words]
            other = m & 1
            if group == 7:
                other = other ^ (m >> 3 & m >> 2 & m >> 1 & 1)
            to_col = ((z + dz) & 3) * 2 + (core ^ other)
            to_row = ((x + dx) & 3) * 4 + ((y + dy) & 3)
            owner = to_col * 16 + to_row
            fill(owner, data, pl.multiple_of(k * 16, 16))
            for copy in transfer(k, owner, group, (to_col, to_row)):
                copy.start()
            return 0

        lax.fori_loop(0, 15 if group == 7 else 16, send, 0)
    fill(me, data_in, 127 * 16)
    own = pltpu.make_async_copy(label.at[pl.ds(me, 1)], label_in.at[pl.ds(127, 1)], table_sem)
    own.start()
    own.wait()

    def build(b, _):
        taps = coef_ref[b * NBASIS] * basis_ref[0]
        for k in range(1, NBASIS):
            taps = taps + coef_ref[b * NBASIS + k] * basis_ref[k]
        for d in range(TAPS):
            i, s = d // GROUP, d % GROUP
            base = pltpu.roll(jnp.broadcast_to(taps[d : d + 1], (8, 128)), 0, 1, stride=1, stride_axis=0)
            spread = jnp.concatenate(
                [pltpu.roll(base, (128 - HALF + q) % 128, 1) for q in range(0, TILE, 8)], axis=0
            )
            weights[b, s * TILE : (s + 1) * TILE, i * 128 : (i + 1) * 128] = spread.astype(jnp.bfloat16)
        return 0

    lax.fori_loop(0, BANDS, build, 0)

    for group in range(8):
        count = 15 if group == 7 else 16
        big = pl.ds(group * 256, count * 16)
        small = pl.ds(group * 16, count)
        pltpu.make_async_remote_copy(
            src_ref=label.at[small], dst_ref=label_in.at[small], send_sem=label_send,
            recv_sem=label_recv.at[group], device_id=(col ^ 1, row), device_id_type=MESH,
        ).wait_recv()
        pltpu.make_async_remote_copy(
            src_ref=data.at[big], dst_ref=data_in.at[big], send_sem=data_send,
            recv_sem=data_recv.at[group], device_id=(col ^ 1, row), device_id_type=MESH,
        ).wait_recv()
        pick = iota((8, 128), 1) >> 4 == iota((8, 128), 0)
        lines = [
            jnp.sum(
                jnp.where(pick, label_in[group * 16 + h * 8 : group * 16 + h * 8 + 8].astype(jnp.float32), 0.0),
                axis=0,
                keepdims=True,
            )
            for h in range(2)
        ]
        line = jnp.concatenate(lines, axis=1).astype(jnp.int32)
        for b in range(BANDS):
            hit = iota((PH, 256), 0) + b * PH == line
            part = jnp.dot(
                hit.astype(jnp.float32).astype(jnp.bfloat16),
                data_in[group * 256 : (group + 1) * 256],
                preferred_element_type=jnp.float32,
            )
            if group:
                sums[b] += part
            else:
                sums[b] = part

    pltpu.make_async_remote_copy(
        src_ref=data.at[pl.ds(0, 127 * 16)], dst_ref=data_in.at[pl.ds(0, 127 * 16)], send_sem=data_send,
        recv_sem=data_recv.at[0], device_id=(col ^ 1, row), device_id_type=MESH,
    ).wait_send()
    pltpu.make_async_remote_copy(
        src_ref=label.at[pl.ds(0, 127)], dst_ref=label_in.at[pl.ds(0, 127)], send_sem=label_send,
        recv_sem=label_recv.at[0], device_id=(col ^ 1, row), device_id_type=MESH,
    ).wait_send()

    lane_p = iota((PH, 128), 1)
    pack_l = jnp.zeros((PH, 128), jnp.float32)
    pack_r = jnp.zeros((PH, 128), jnp.float32)
    for b in range(BANDS):
        mean = sums[b, :, 0:PW] / jnp.maximum(sums[b, :, PW : 2 * PW], 1.0)
        sums[b, :, 0:PW] = mean
        mean_b[b] = mean.astype(jnp.bfloat16)
        here = (lane_p >= b * HALF) & (lane_p < (b + 1) * HALF)
        pack_l = jnp.where(here, pltpu.roll(mean[:, 0:128], b * HALF, 1), pack_l)
        pack_r = jnp.where(here, pltpu.roll(mean[:, 128:256], (b * HALF + HALF) % 128, 1), pack_r)
    packs[0] = pack_l.astype(jnp.bfloat16)
    packs[1] = pack_r.astype(jnp.bfloat16)

    up, down = (row + 15) & 15, (row + 1) & 15
    left, right = (col + 7) & 7, (col + 1) & 7
    routes = (
        (mean_b.at[:, PH - 32 : PH], above, (col, down)),
        (mean_b.at[:, 0:32], below, (col, up)),
        (packs.at[0], side_r.at[32 : 32 + PH], (left, row)),
        (packs.at[1], side_l.at[32 : 32 + PH], (right, row)),
        (packs.at[0, PH - 32 : PH], side_r.at[0:32], (left, down)),
        (packs.at[1, PH - 32 : PH], side_l.at[0:32], (right, down)),
        (packs.at[0, 0:32], side_r.at[32 + PH : ROWS], (left, up)),
        (packs.at[1, 0:32], side_l.at[32 + PH : ROWS], (right, up)),
    )
    halos = [
        pltpu.make_async_remote_copy(
            src_ref=src, dst_ref=dst, send_sem=halo_send.at[i], recv_sem=halo_recv.at[i],
            device_id=target, device_id_type=MESH,
        )
        for i, (src, dst, target) in enumerate(routes)
    ]
    for halo in halos:
        halo.start()
    for halo in halos:
        halo.wait()

    lane_r = iota((ROWS, 128), 1)
    sub_r = iota((ROWS, 128), 0)
    has_up, has_down, has_left, has_right = row > 0, row < 15, col > 0, col < 7
    live = jnp.where(has_up, 0, 32), jnp.where(has_down, ROWS, ROWS - 32)
    inside = (sub_r >= live[0]) & (sub_r < live[1])
    lane_o = iota((PH, 128), 1)

    def convolve(b, _):
        top = jnp.where(has_up, above[b].astype(jnp.float32), 0.0)
        bottom = jnp.where(has_down, below[b].astype(jnp.float32), 0.0)
        full = jnp.concatenate([top, sums[b, :, 0:PW], bottom], axis=0)
        tile0, tile1 = full[:, 0:128], full[:, 128:256]
        back = 128 - b * HALF
        edge_l = pltpu.roll(side_l[...].astype(jnp.float32), (back + 108) & 127, 1)
        edge_r = pltpu.roll(side_r[...].astype(jnp.float32), back & 127, 1)
        edge_l = jnp.where(inside & has_left, edge_l, 0.0)
        edge_r = jnp.where(inside & has_right, edge_r, 0.0)
        windows = (
            jnp.where(lane_r < 108, tile0, edge_l),
            pltpu.roll(jnp.where(lane_r < 32, tile1, tile0), 64, 1),
            jnp.where(lane_r < 108, tile1, tile0),
            pltpu.roll(jnp.where(lane_r < 32, edge_r, tile1), 64, 1),
        )
        for a, window in enumerate(windows):
            image32[pl.ds(a, ROWS, stride=4), :] = window
        low = image32[0 : 4 * ROWS].astype(jnp.bfloat16)
        image2[:, 0:128] = low
        image2[0 : 4 * ROWS - 16, 128:256] = low[16:]
        left_side = jnp.concatenate(
            [image2[4 * FIRST + 32 * p : 4 * FIRST + 32 * p + OUT_ROWS] for p in range(SHIFTS // 2)], axis=1
        )
        full_prod = lax.dot_general(
            left_side, weights[b], (((1,), (1,)), ((), ())), preferred_element_type=jnp.float32
        )
        prod[0 : OUT_ROWS - 8] = full_prod[0 : OUT_ROWS - 8, 0:128] + full_prod[8:OUT_ROWS, 128:256]
        for h in range(2):
            e0 = prod[pl.ds(2 * h, PH, stride=4), :]
            e0n = prod[pl.ds(2 * h + 4, PH, stride=4), :]
            e1 = prod[pl.ds(2 * h + 1, PH, stride=4), :]
            e1n = prod[pl.ds(2 * h + 5, PH, stride=4), :]
            kept = jnp.where(lane_o < TILE, e0, e1n)
            moved = jnp.where(lane_o < TILE, e1, e0n)
            out_v[b, :, h * 128 : (h + 1) * 128] = kept + pltpu.roll(moved, TILE, 1)
        return 0

    lax.fori_loop(0, BANDS, convolve, 0)
    result = pltpu.make_async_copy(out_v, out_hbm, out_sem)
    result.start()
    result.wait()


def on_device(
    block_pixels,
    block_ivar,
    block_mask,
    block_patch,
    block_offset,
    block_exposure,
    exposure_band,
    basis,
    coefficients,
):
    f32, bf16, i32 = jnp.float32, jnp.bfloat16, jnp.int32
    lines = [block_patch.reshape(1, 128), block_offset.reshape(1, 128), block_exposure.reshape(1, 128)]
    lines.append(jnp.pad(exposure_band, (0, 128 - exposure_band.shape[0])).reshape(1, 128))
    taps = jnp.pad(basis, ((0, 0), (0, TAPS - KS), (0, 128 - KS)))
    vmem, smem, hbm = pltpu.VMEM, pltpu.SMEM, pl.ANY
    dma = pltpu.SemaphoreType.DMA
    return pl.pallas_call(
        body,
        out_shape=jax.ShapeDtypeStruct((BANDS, PH, PW), f32),
        in_specs=[pl.BlockSpec(memory_space=smem)]
        + [pl.BlockSpec(memory_space=vmem)] * 5
        + [pl.BlockSpec(memory_space=hbm)] * 3,
        out_specs=pl.BlockSpec(memory_space=hbm),
        scratch_shapes=[
            vmem((128, BH, PW), f32),
            vmem((128, BH, PW), bf16),
            vmem((128, BH, PW), i32),
            vmem((8, 128), i32),
            smem((8, 128), i32),
            vmem((128, 128), i32),
            vmem((128, 128), i32),
            vmem((2048, 2 * PW), bf16),
            vmem((2048, 2 * PW), bf16),
            vmem((BANDS, PH, 2 * PW), f32),
            vmem((BANDS, GROUP * TILE, SHIFTS * 128), bf16),
            vmem((BANDS, PH, PW), bf16),
            vmem((2, PH, 128), bf16),
            vmem((BANDS, 32, PW), bf16),
            vmem((BANDS, 32, PW), bf16),
            vmem((ROWS, 128), bf16),
            vmem((ROWS, 128), bf16),
            vmem((4 * ROWS + 8, 128), f32),
            vmem((4 * ROWS, 256), bf16),
            vmem((OUT_ROWS, 128), f32),
            vmem((BANDS, PH, PW), f32),
            dma((3,)),
            dma,
            dma,
            dma((8,)),
            dma,
            dma((8,)),
            dma((8,)),
            dma((8,)),
            dma,
        ],
        compiler_params=pltpu.CompilerParams(
            collective_id=0, has_side_effects=True, vmem_limit_bytes=48 << 20
        ),
        cost_estimate=pl.CostEstimate(flops=6 << 30, bytes_accessed=4 << 20, transcendentals=0),
    )(coefficients.reshape(BANDS * NBASIS), *lines, taps, block_pixels, block_ivar, block_mask)


def solution(mesh):
    placed = (
        P(("col", "row"), None, None),
        P(("col", "row"), None, None),
        P(("col", "row"), None, None),
        P(("col", "row"), None),
        P(("col", "row")),
        P(("col", "row")),
        P(),
        P(),
        P("row", "col", None, None),
    )
    return jax.shard_map(
        on_device, mesh=mesh, in_specs=placed, out_specs=P(None, "row", "col"), check_vma=False
    )
```

```python
import jax
import jax.numpy as jnp
from jax import lax
from jax.experimental import pallas as pl
from jax.experimental.pallas import tpu as pltpu
from jax.sharding import PartitionSpec as P

BANDS = 6
NBASIS = 5
KS = 41
HALF = 20
PH = 128
PW = 256
BH = 8
MESH = pl.DeviceIdType.MESH

STEP_X = (-1782682714, -1921033681, 1934304481, 809635604)
STEP_Y = (1734851178, 1843253947, 483576120, 202408901)
STEP_Z = (1524231834, 502626494, -985886066, 50605265)

GROUP = 4
TILE = 64
TAPS = 48
SHIFTS = TAPS // GROUP
ROWS = PH + 64
FIRST = 32 - HALF
OUT_ROWS = 528


def iota(shape, dim):
    return lax.broadcasted_iota(jnp.int32, shape, dim)


def body(
    pix_hbm,
    ivar_hbm,
    mask_hbm,
    patch_hbm,
    offset_hbm,
    exposure_hbm,
    band_hbm,
    basis_hbm,
    coef_hbm,
    out_hbm,
    pix,
    ivar,
    mask,
    patch_ref,
    offset_ref,
    exposure_ref,
    band_ref,
    basis_ref,
    coef_ref,
    taps_ref,
    table,
    table_s,
    label,
    label_in,
    data,
    data_in,
    sums,
    weights,
    mean_b,
    packs,
    above,
    below,
    side_l,
    side_r,
    image32,
    image2,
    prod,
    out_v,
    in_sem,
    table_sem,
    data_send,
    data_recv,
    label_send,
    label_recv,
    halo_send,
    halo_recv,
    out_sem,
):
    col = lax.axis_index("col")
    row = lax.axis_index("row")
    me = col * 16 + row
    z, core, x, y = col >> 1, col & 1, row >> 2, row & 3

    loads = [
        pltpu.make_async_copy(src, dst, in_sem.at[i])
        for i, (src, dst) in enumerate(
            (
                (patch_hbm, patch_ref),
                (offset_hbm, offset_ref),
                (exposure_hbm, exposure_ref),
                (band_hbm, band_ref),
                (pix_hbm, pix),
                (ivar_hbm, ivar),
                (mask_hbm, mask),
                (basis_hbm, basis_ref),
                (coef_hbm, coef_ref),
            )
        )
    ]
    barrier = pltpu.get_barrier_semaphore()

    def greet(k, _):
        peer = (me + k) & 127
        pl.semaphore_signal(barrier, inc=1, device_id=(peer >> 4, peer & 15), device_id_type=MESH)
        return 0

    lax.fori_loop(1, 128, greet, 0)
    for load in loads:
        load.start()
    for load in loads[:4]:
        load.wait()

    square = (128, 128)
    sub, lane = iota(square, 0), iota(square, 1)
    diag = sub == lane

    def to_column(line):
        return jnp.sum(jnp.where(diag, line, 0.0), axis=1, keepdims=True)

    def to_line(column):
        return jnp.sum(jnp.where(diag, column, 0.0), axis=0, keepdims=True)

    subf, lanef = sub.astype(jnp.float32), lane.astype(jnp.float32)
    patch = patch_ref[...].astype(jnp.float32)
    exposures = band_ref.shape[1]
    band_line = jnp.broadcast_to(band_ref[...].astype(jnp.float32), (exposures, exposures))
    band_col = jnp.sum(
        jnp.where(iota(band_line.shape, 0) == iota(band_line.shape, 1), band_line, 0.0), axis=1, keepdims=True
    )
    band_line = jnp.sum(
        jnp.where(exposure_ref[...].astype(jnp.float32) == subf[0:exposures], band_col, 0.0), axis=0, keepdims=True
    )
    key_line = band_line * float(PH) + offset_ref[...].astype(jnp.float32)
    named = patch == subf
    low = jnp.min(jnp.where(named, lanef, 128.0), axis=1, keepdims=True)
    high = jnp.max(jnp.where(named, lanef, -1.0), axis=1, keepdims=True)
    key_low = jnp.sum(jnp.where(lanef == low, key_line, 0.0), axis=1, keepdims=True)
    key_high = jnp.sum(jnp.where(lanef == high, key_line, 0.0), axis=1, keepdims=True)
    key_low = jnp.where(low < 128.0, key_low, -1000.0)
    key_high = jnp.where(high > low, key_high, -1000.0)
    place = (lane & 15) < BH
    label[...] = (jnp.where(place, key_low, key_high) + (lane & 7).astype(jnp.float32)).astype(jnp.int32)
    low_line = to_line(jnp.minimum(low, 127.0))
    high_line = to_line(jnp.maximum(high, 0.0))
    table[...] = jnp.where(iota((8, 128), 0) == 0, low_line, high_line).astype(jnp.int32)
    to_smem = pltpu.make_async_copy(table, table_s, table_sem)
    to_smem.start()
    to_smem.wait()

    for load in loads[4:]:
        load.wait()
    pl.semaphore_wait(barrier, 127)

    def fill(owner, into, at):
        first, second = table_s[0, owner] & 127, table_s[1, owner] & 127
        w0 = mask[first].astype(jnp.float32) * ivar[first].astype(jnp.float32)
        w1 = mask[second].astype(jnp.float32) * ivar[second].astype(jnp.float32)
        p0, p1 = w0 * pix[first], w1 * pix[second]
        into[pl.ds(at, 16), 0:PW] = jnp.concatenate([p0, p1], axis=0).astype(jnp.bfloat16)
        into[pl.ds(at, 16), PW : 2 * PW] = jnp.concatenate([w0, w1], axis=0).astype(jnp.bfloat16)

    def transfer(k, owner, group, target):
        rows = pl.ds(pl.multiple_of(k * 16, 16), 16)
        return (
            pltpu.make_async_remote_copy(
                src_ref=data.at[rows],
                dst_ref=data_in.at[rows],
                send_sem=data_send,
                recv_sem=data_recv.at[group],
                device_id=target,
                device_id_type=MESH,
            ),
            pltpu.make_async_remote_copy(
                src_ref=label.at[pl.ds(owner, 1)],
                dst_ref=label_in.at[pl.ds(k, 1)],
                send_sem=label_send,
                recv_sem=label_recv.at[group],
                device_id=target,
                device_id_type=MESH,
            ),
        )

    for group in range(8):
        words = [steps[group >> 1] for steps in (STEP_X, STEP_Y, STEP_Z)]

        def send(m, _, group=group, words=words):
            k = group * 16 + m
            shift = ((group & 1) * 8 + (m >> 1)) * 2
            dx, dy, dz = [(jnp.int32(word) >> shift) & 3 for word in words]
            other = m & 1
            if group == 7:
                other = other ^ (m >> 3 & m >> 2 & m >> 1 & 1)
            to_col = ((z + dz) & 3) * 2 + (core ^ other)
            to_row = ((x + dx) & 3) * 4 + ((y + dy) & 3)
            owner = to_col * 16 + to_row
            fill(owner, data, pl.multiple_of(k * 16, 16))
            for copy in transfer(k, owner, group, (to_col, to_row)):
                copy.start()
            return 0

        lax.fori_loop(0, 15 if group == 7 else 16, send, 0)
    fill(me, data_in, 127 * 16)
    own = pltpu.make_async_copy(label.at[pl.ds(me, 1)], label_in.at[pl.ds(127, 1)], table_sem)
    own.start()
    own.wait()

    taps_ref[...] = jnp.zeros_like(taps_ref)

    def build(b, _):
        combined = coef_ref[0, 0, 0, b] * basis_ref[0]
        for k in range(1, NBASIS):
            combined = combined + coef_ref[0, k, 0, b] * basis_ref[k]
        taps_ref[0:KS, 0:KS] = combined
        taps = taps_ref[...]
        for d in range(TAPS):
            i, s = d // GROUP, d % GROUP
            base = pltpu.roll(jnp.broadcast_to(taps[d : d + 1], (8, 128)), 0, 1, stride=1, stride_axis=0)
            spread = jnp.concatenate(
                [pltpu.roll(base, (128 - HALF + q) % 128, 1) for q in range(0, TILE, 8)], axis=0
            )
            weights[b, s * TILE : (s + 1) * TILE, i * 128 : (i + 1) * 128] = spread.astype(jnp.bfloat16)
        return 0

    lax.fori_loop(0, BANDS, build, 0)

    for group in range(8):
        count = 15 if group == 7 else 16
        big = pl.ds(group * 256, count * 16)
        small = pl.ds(group * 16, count)
        pltpu.make_async_remote_copy(
            src_ref=label.at[small], dst_ref=label_in.at[small], send_sem=label_send,
            recv_sem=label_recv.at[group], device_id=(col ^ 1, row), device_id_type=MESH,
        ).wait_recv()
        pltpu.make_async_remote_copy(
            src_ref=data.at[big], dst_ref=data_in.at[big], send_sem=data_send,
            recv_sem=data_recv.at[group], device_id=(col ^ 1, row), device_id_type=MESH,
        ).wait_recv()
        pick = iota((8, 128), 1) >> 4 == iota((8, 128), 0)
        lines = [
            jnp.sum(
                jnp.where(pick, label_in[group * 16 + h * 8 : group * 16 + h * 8 + 8].astype(jnp.float32), 0.0),
                axis=0,
                keepdims=True,
            )
            for h in range(2)
        ]
        line = jnp.concatenate(lines, axis=1).astype(jnp.int32)
        for b in range(BANDS):
            hit = iota((PH, 256), 0) + b * PH == line
            part = jnp.dot(
                hit.astype(jnp.float32).astype(jnp.bfloat16),
                data_in[group * 256 : (group + 1) * 256],
                preferred_element_type=jnp.float32,
            )
            if group:
                sums[b] += part
            else:
                sums[b] = part

    pltpu.make_async_remote_copy(
        src_ref=data.at[pl.ds(0, 127 * 16)], dst_ref=data_in.at[pl.ds(0, 127 * 16)], send_sem=data_send,
        recv_sem=data_recv.at[0], device_id=(col ^ 1, row), device_id_type=MESH,
    ).wait_send()
    pltpu.make_async_remote_copy(
        src_ref=label.at[pl.ds(0, 127)], dst_ref=label_in.at[pl.ds(0, 127)], send_sem=label_send,
        recv_sem=label_recv.at[0], device_id=(col ^ 1, row), device_id_type=MESH,
    ).wait_send()

    lane_p = iota((PH, 128), 1)
    pack_l = jnp.zeros((PH, 128), jnp.float32)
    pack_r = jnp.zeros((PH, 128), jnp.float32)
    for b in range(BANDS):
        mean = sums[b, :, 0:PW] / jnp.maximum(sums[b, :, PW : 2 * PW], 1.0)
        sums[b, :, 0:PW] = mean
        mean_b[b] = mean.astype(jnp.bfloat16)
        here = (lane_p >= b * HALF) & (lane_p < (b + 1) * HALF)
        pack_l = jnp.where(here, pltpu.roll(mean[:, 0:128], b * HALF, 1), pack_l)
        pack_r = jnp.where(here, pltpu.roll(mean[:, 128:256], (b * HALF + HALF) % 128, 1), pack_r)
    packs[0] = pack_l.astype(jnp.bfloat16)
    packs[1] = pack_r.astype(jnp.bfloat16)

    up, down = (row + 15) & 15, (row + 1) & 15
    left, right = (col + 7) & 7, (col + 1) & 7
    routes = (
        (mean_b.at[:, PH - 32 : PH], above, (col, down)),
        (mean_b.at[:, 0:32], below, (col, up)),
        (packs.at[0], side_r.at[32 : 32 + PH], (left, row)),
        (packs.at[1], side_l.at[32 : 32 + PH], (right, row)),
        (packs.at[0, PH - 32 : PH], side_r.at[0:32], (left, down)),
        (packs.at[1, PH - 32 : PH], side_l.at[0:32], (right, down)),
        (packs.at[0, 0:32], side_r.at[32 + PH : ROWS], (left, up)),
        (packs.at[1, 0:32], side_l.at[32 + PH : ROWS], (right, up)),
    )
    halos = [
        pltpu.make_async_remote_copy(
            src_ref=src, dst_ref=dst, send_sem=halo_send.at[i], recv_sem=halo_recv.at[i],
            device_id=target, device_id_type=MESH,
        )
        for i, (src, dst, target) in enumerate(routes)
    ]
    for halo in halos:
        halo.start()
    for halo in halos:
        halo.wait()

    lane_r = iota((ROWS, 128), 1)
    sub_r = iota((ROWS, 128), 0)
    has_up, has_down, has_left, has_right = row > 0, row < 15, col > 0, col < 7
    live = jnp.where(has_up, 0, 32), jnp.where(has_down, ROWS, ROWS - 32)
    inside = (sub_r >= live[0]) & (sub_r < live[1])
    lane_o = iota((PH, 128), 1)

    def convolve(b, _):
        top = jnp.where(has_up, above[b].astype(jnp.float32), 0.0)
        bottom = jnp.where(has_down, below[b].astype(jnp.float32), 0.0)
        full = jnp.concatenate([top, sums[b, :, 0:PW], bottom], axis=0)
        tile0, tile1 = full[:, 0:128], full[:, 128:256]
        back = 128 - b * HALF
        edge_l = pltpu.roll(side_l[...].astype(jnp.float32), (back + 108) & 127, 1)
        edge_r = pltpu.roll(side_r[...].astype(jnp.float32), back & 127, 1)
        edge_l = jnp.where(inside & has_left, edge_l, 0.0)
        edge_r = jnp.where(inside & has_right, edge_r, 0.0)
        windows = (
            jnp.where(lane_r < 108, tile0, edge_l),
            pltpu.roll(jnp.where(lane_r < 32, tile1, tile0), 64, 1),
            jnp.where(lane_r < 108, tile1, tile0),
            pltpu.roll(jnp.where(lane_r < 32, edge_r, tile1), 64, 1),
        )
        for a, window in enumerate(windows):
            image32[pl.ds(a, ROWS, stride=4), :] = window
        low = image32[0 : 4 * ROWS].astype(jnp.bfloat16)
        image2[:, 0:128] = low
        image2[0 : 4 * ROWS - 16, 128:256] = low[16:]
        left_side = jnp.concatenate(
            [image2[4 * FIRST + 32 * p : 4 * FIRST + 32 * p + OUT_ROWS] for p in range(SHIFTS // 2)], axis=1
        )
        full_prod = lax.dot_general(
            left_side, weights[b], (((1,), (1,)), ((), ())), preferred_element_type=jnp.float32
        )
        prod[0 : OUT_ROWS - 8] = full_prod[0 : OUT_ROWS - 8, 0:128] + full_prod[8:OUT_ROWS, 128:256]
        for h in range(2):
            e0 = prod[pl.ds(2 * h, PH, stride=4), :]
            e0n = prod[pl.ds(2 * h + 4, PH, stride=4), :]
            e1 = prod[pl.ds(2 * h + 1, PH, stride=4), :]
            e1n = prod[pl.ds(2 * h + 5, PH, stride=4), :]
            kept = jnp.where(lane_o < TILE, e0, e1n)
            moved = jnp.where(lane_o < TILE, e1, e0n)
            out_v[b, :, h * 128 : (h + 1) * 128] = kept + pltpu.roll(moved, TILE, 1)
        return 0

    lax.fori_loop(0, BANDS, convolve, 0)
    result = pltpu.make_async_copy(out_v, out_hbm, out_sem)
    result.start()
    result.wait()


def on_device(
    block_pixels,
    block_ivar,
    block_mask,
    block_patch,
    block_offset,
    block_exposure,
    exposure_band,
    basis,
    coefficients,
):
    f32, bf16, i32 = jnp.float32, jnp.bfloat16, jnp.int32
    lines = [v.reshape(1, v.size) for v in (block_patch, block_offset, block_exposure, exposure_band)]
    scales = coefficients.transpose(0, 3, 1, 2)
    vmem, smem, hbm = pltpu.VMEM, pltpu.SMEM, pltpu.HBM
    dma = pltpu.SemaphoreType.DMA
    return pl.pallas_call(
        body,
        out_shape=jax.ShapeDtypeStruct((BANDS, PH, PW), f32),
        in_specs=[pl.BlockSpec(memory_space=hbm)] * 9,
        out_specs=pl.BlockSpec(memory_space=hbm),
        scratch_shapes=[
            vmem((128, BH, PW), f32),
            vmem((128, BH, PW), bf16),
            vmem((128, BH, PW), i32),
            vmem((1, 128), i32),
            vmem((1, 128), i32),
            vmem((1, 128), i32),
            vmem((1, exposure_band.size), i32),
            vmem(basis.shape, f32),
            smem(scales.shape, f32),
            vmem((TAPS, 128), f32),
            vmem((8, 128), i32),
            smem((8, 128), i32),
            vmem((128, 128), i32),
            vmem((128, 128), i32),
            vmem((2048, 2 * PW), bf16),
            vmem((2048, 2 * PW), bf16),
            vmem((BANDS, PH, 2 * PW), f32),
            vmem((BANDS, GROUP * TILE, SHIFTS * 128), bf16),
            vmem((BANDS, PH, PW), bf16),
            vmem((2, PH, 128), bf16),
            vmem((BANDS, 32, PW), bf16),
            vmem((BANDS, 32, PW), bf16),
            vmem((ROWS, 128), bf16),
            vmem((ROWS, 128), bf16),
            vmem((4 * ROWS + 8, 128), f32),
            vmem((4 * ROWS, 256), bf16),
            vmem((OUT_ROWS, 128), f32),
            vmem((BANDS, PH, PW), f32),
            dma((9,)),
            dma,
            dma,
            dma((8,)),
            dma,
            dma((8,)),
            dma((8,)),
            dma((8,)),
            dma,
        ],
        compiler_params=pltpu.CompilerParams(
            collective_id=0, has_side_effects=True, vmem_limit_bytes=56 << 20
        ),
        cost_estimate=pl.CostEstimate(flops=6 << 30, bytes_accessed=4 << 20, transcendentals=0),
    )(block_pixels, block_ivar, block_mask, *lines, basis, scales)


def solution(mesh):
    placed = (
        P(("col", "row"), None, None),
        P(("col", "row"), None, None),
        P(("col", "row"), None, None),
        P(("col", "row"), None),
        P(("col", "row")),
        P(("col", "row")),
        P(),
        P(),
        P("row", "col", None, None),
    )
    return jax.shard_map(
        on_device, mesh=mesh, in_specs=placed, out_specs=P(None, "row", "col"), check_vma=False
    )
```

```python
import jax
import jax.numpy as jnp
from jax import lax
from jax.experimental import pallas as pl
from jax.experimental.pallas import tpu as pltpu
from jax.sharding import PartitionSpec as P

BANDS = 6
NBASIS = 5
KS = 41
HALF = 20
PH = 128
PW = 256
BH = 8
MESH = pl.DeviceIdType.MESH

STEP_X = (-2134884224, -1862789622, 1547504322, -997211824, 1521461850, -1521111046, -2790657, 930528599)
STEP_Y = (-1473245152, 621707680, 130240700, 824245269, -1347790166, 1516198495, 2105372591, 904625533)
STEP_Z = (672072970, 1252255834, -246087895, 998725, -84236886, 1437267365, -715665414, 15743)
STEP_C = (285475844, 71372868, 1091585041, 1431572740, 1145324612, 1145324612, 286331972, 357912849)
LINES, PLANES = 13, 64

GROUP = 4
TILE = 64
TAPS = 48
SHIFTS = TAPS // GROUP
ROWS = PH + 64
FIRST = 32 - HALF
OUT_ROWS = 528


def iota(shape, dim):
    return lax.broadcasted_iota(jnp.int32, shape, dim)


def body(
    pix_hbm,
    ivar_hbm,
    mask_hbm,
    patch_hbm,
    offset_hbm,
    exposure_hbm,
    band_hbm,
    basis_hbm,
    coef_hbm,
    out_hbm,
    pix,
    ivar,
    mask,
    patch_ref,
    offset_ref,
    exposure_ref,
    band_ref,
    basis_ref,
    coef_ref,
    taps_ref,
    table,
    table_s,
    label,
    label_in,
    data,
    data_in,
    sums,
    weights,
    mean_b,
    packs,
    above,
    below,
    side_l,
    side_r,
    image32,
    image2,
    prod,
    out_v,
    in_sem,
    table_sem,
    data_send,
    data_recv,
    label_send,
    label_recv,
    halo_send,
    halo_recv,
    out_sem,
    line_sem,
    plane_sem,
):
    col = lax.axis_index("col")
    row = lax.axis_index("row")
    me = col * 16 + row
    z, core, x, y = col >> 1, col & 1, row >> 2, row & 3

    loads = [
        pltpu.make_async_copy(src, dst, in_sem.at[i])
        for i, (src, dst) in enumerate(
            (
                (patch_hbm, patch_ref),
                (offset_hbm, offset_ref),
                (exposure_hbm, exposure_ref),
                (band_hbm, band_ref),
                (pix_hbm, pix),
                (ivar_hbm, ivar),
                (mask_hbm, mask),
                (basis_hbm, basis_ref),
                (coef_hbm, coef_ref),
            )
        )
    ]
    barrier = pltpu.get_barrier_semaphore()
    on_line = (
        [((col + d) & 7, row) for d in range(1, 8)]
        + [(col, x * 4 + ((y + d) & 3)) for d in range(1, 4)]
        + [(col, ((x + d) & 3) * 4 + y) for d in range(1, 4)]
    )
    for peer in on_line:
        pl.semaphore_signal(barrier, inc=1, device_id=peer, device_id_type=MESH)
    for load in loads:
        load.start()
    for load in loads[:4]:
        load.wait()

    square = (128, 128)
    sub, lane = iota(square, 0), iota(square, 1)
    diag = sub == lane

    def to_column(line):
        return jnp.sum(jnp.where(diag, line, 0.0), axis=1, keepdims=True)

    def to_line(column):
        return jnp.sum(jnp.where(diag, column, 0.0), axis=0, keepdims=True)

    subf, lanef = sub.astype(jnp.float32), lane.astype(jnp.float32)
    patch = patch_ref[...].astype(jnp.float32)
    exposures = band_ref.shape[1]
    band_line = jnp.broadcast_to(band_ref[...].astype(jnp.float32), (exposures, exposures))
    band_col = jnp.sum(
        jnp.where(iota(band_line.shape, 0) == iota(band_line.shape, 1), band_line, 0.0), axis=1, keepdims=True
    )
    band_line = jnp.sum(
        jnp.where(exposure_ref[...].astype(jnp.float32) == subf[0:exposures], band_col, 0.0), axis=0, keepdims=True
    )
    key_line = band_line * float(PH) + offset_ref[...].astype(jnp.float32)
    named = patch == subf
    low = jnp.min(jnp.where(named, lanef, 128.0), axis=1, keepdims=True)
    high = jnp.max(jnp.where(named, lanef, -1.0), axis=1, keepdims=True)
    key_low = jnp.sum(jnp.where(lanef == low, key_line, 0.0), axis=1, keepdims=True)
    key_high = jnp.sum(jnp.where(lanef == high, key_line, 0.0), axis=1, keepdims=True)
    key_low = jnp.where(low < 128.0, key_low, -1000.0)
    key_high = jnp.where(high > low, key_high, -1000.0)
    place = (lane & 15) < BH
    label[...] = (jnp.where(place, key_low, key_high) + (lane & 7).astype(jnp.float32)).astype(jnp.int32)
    low_line = to_line(jnp.minimum(low, 127.0))
    high_line = to_line(jnp.maximum(high, 0.0))
    table[...] = jnp.where(iota((8, 128), 0) == 0, low_line, high_line).astype(jnp.int32)
    to_smem = pltpu.make_async_copy(table, table_s, table_sem)
    to_smem.start()
    to_smem.wait()

    for load in loads[4:]:
        load.wait()

    def fill(owner, into, at):
        first, second = table_s[0, owner] & 127, table_s[1, owner] & 127
        w0 = mask[first].astype(jnp.float32) * ivar[first].astype(jnp.float32)
        w1 = mask[second].astype(jnp.float32) * ivar[second].astype(jnp.float32)
        p0, p1 = w0 * pix[first], w1 * pix[second]
        into[pl.ds(at, 16), 0:PW] = jnp.concatenate([p0, p1], axis=0).astype(jnp.bfloat16)
        into[pl.ds(at, 16), PW : 2 * PW] = jnp.concatenate([w0, w1], axis=0).astype(jnp.bfloat16)

    def transfer(k, owner, group, target):
        rows = pl.ds(pl.multiple_of(k * 16, 16), 16)
        return (
            pltpu.make_async_remote_copy(
                src_ref=data.at[rows],
                dst_ref=data_in.at[rows],
                send_sem=data_send,
                recv_sem=data_recv.at[group],
                device_id=target,
                device_id_type=MESH,
            ),
            pltpu.make_async_remote_copy(
                src_ref=label.at[pl.ds(owner, 1)],
                dst_ref=label_in.at[pl.ds(k, 1)],
                send_sem=label_send,
                recv_sem=label_recv.at[group],
                device_id=target,
                device_id_type=MESH,
            ),
        )

    def send_some(first, last):
        group = first // 16
        words = [steps[group] for steps in (STEP_X, STEP_Y, STEP_Z, STEP_C)]

        def send(m, _):
            k = group * 16 + m
            dx, dy, dz, dc = [(jnp.int32(word) >> (2 * m)) & 3 for word in words]
            to_col = ((z + dz) & 3) * 2 + (core ^ dc)
            to_row = ((x + dx) & 3) * 4 + ((y + dy) & 3)
            owner = to_col * 16 + to_row
            fill(owner, data, pl.multiple_of(k * 16, 16))
            for copy in transfer(k, owner, group, (to_col, to_row)):
                copy.start()
            return 0

        lax.fori_loop(first - group * 16, last - group * 16, send, 0)

    pl.semaphore_wait(barrier, len(on_line))
    for peer in on_line:
        pl.semaphore_signal(line_sem, inc=1, device_id=peer, device_id_type=MESH)
    send_some(0, LINES)
    pl.semaphore_wait(line_sem, len(on_line))
    for peer in on_line[-3:]:
        pl.semaphore_signal(plane_sem, inc=1, device_id=peer, device_id_type=MESH)
    send_some(LINES, 16)
    for first in range(16, PLANES, 16):
        send_some(first, first + 16)
    pl.semaphore_wait(plane_sem, 3)
    for first in range(PLANES, 128, 16):
        send_some(first, min(first + 16, 127))
    fill(me, data_in, 127 * 16)
    own = pltpu.make_async_copy(label.at[pl.ds(me, 1)], label_in.at[pl.ds(127, 1)], table_sem)
    own.start()
    own.wait()

    taps_ref[...] = jnp.zeros_like(taps_ref)

    def build(b, _):
        combined = coef_ref[0, 0, 0, b] * basis_ref[0]
        for k in range(1, NBASIS):
            combined = combined + coef_ref[0, k, 0, b] * basis_ref[k]
        taps_ref[0:KS, 0:KS] = combined
        taps = taps_ref[...]
        for d in range(TAPS):
            i, s = d // GROUP, d % GROUP
            base = pltpu.roll(jnp.broadcast_to(taps[d : d + 1], (8, 128)), 0, 1, stride=1, stride_axis=0)
            spread = jnp.concatenate(
                [pltpu.roll(base, (128 - HALF + q) % 128, 1) for q in range(0, TILE, 8)], axis=0
            )
            weights[b, s * TILE : (s + 1) * TILE, i * 128 : (i + 1) * 128] = spread.astype(jnp.bfloat16)
        return 0

    lax.fori_loop(0, BANDS, build, 0)

    for group in range(8):
        count = 15 if group == 7 else 16
        big = pl.ds(group * 256, count * 16)
        small = pl.ds(group * 16, count)
        pltpu.make_async_remote_copy(
            src_ref=label.at[small], dst_ref=label_in.at[small], send_sem=label_send,
            recv_sem=label_recv.at[group], device_id=(col ^ 1, row), device_id_type=MESH,
        ).wait_recv()
        pltpu.make_async_remote_copy(
            src_ref=data.at[big], dst_ref=data_in.at[big], send_sem=data_send,
            recv_sem=data_recv.at[group], device_id=(col ^ 1, row), device_id_type=MESH,
        ).wait_recv()
        pick = iota((8, 128), 1) >> 4 == iota((8, 128), 0)
        lines = [
            jnp.sum(
                jnp.where(pick, label_in[group * 16 + h * 8 : group * 16 + h * 8 + 8].astype(jnp.float32), 0.0),
                axis=0,
                keepdims=True,
            )
            for h in range(2)
        ]
        line = jnp.concatenate(lines, axis=1).astype(jnp.int32)
        for b in range(BANDS):
            hit = iota((PH, 256), 0) + b * PH == line
            part = jnp.dot(
                hit.astype(jnp.float32).astype(jnp.bfloat16),
                data_in[group * 256 : (group + 1) * 256],
                preferred_element_type=jnp.float32,
            )
            if group:
                sums[b] += part
            else:
                sums[b] = part

    pltpu.make_async_remote_copy(
        src_ref=data.at[pl.ds(0, 127 * 16)], dst_ref=data_in.at[pl.ds(0, 127 * 16)], send_sem=data_send,
        recv_sem=data_recv.at[0], device_id=(col ^ 1, row), device_id_type=MESH,
    ).wait_send()
    pltpu.make_async_remote_copy(
        src_ref=label.at[pl.ds(0, 127)], dst_ref=label_in.at[pl.ds(0, 127)], send_sem=label_send,
        recv_sem=label_recv.at[0], device_id=(col ^ 1, row), device_id_type=MESH,
    ).wait_send()

    lane_p = iota((PH, 128), 1)
    pack_l = jnp.zeros((PH, 128), jnp.float32)
    pack_r = jnp.zeros((PH, 128), jnp.float32)
    for b in range(BANDS):
        mean = sums[b, :, 0:PW] / jnp.maximum(sums[b, :, PW : 2 * PW], 1.0)
        sums[b, :, 0:PW] = mean
        mean_b[b] = mean.astype(jnp.bfloat16)
        here = (lane_p >= b * HALF) & (lane_p < (b + 1) * HALF)
        pack_l = jnp.where(here, pltpu.roll(mean[:, 0:128], b * HALF, 1), pack_l)
        pack_r = jnp.where(here, pltpu.roll(mean[:, 128:256], (b * HALF + HALF) % 128, 1), pack_r)
    packs[0] = pack_l.astype(jnp.bfloat16)
    packs[1] = pack_r.astype(jnp.bfloat16)

    up, down = (row + 15) & 15, (row + 1) & 15
    left, right = (col + 7) & 7, (col + 1) & 7
    routes = (
        (mean_b.at[:, PH - 32 : PH], above, (col, down)),
        (mean_b.at[:, 0:32], below, (col, up)),
        (packs.at[0], side_r.at[32 : 32 + PH], (left, row)),
        (packs.at[1], side_l.at[32 : 32 + PH], (right, row)),
        (packs.at[0, PH - 32 : PH], side_r.at[0:32], (left, down)),
        (packs.at[1, PH - 32 : PH], side_l.at[0:32], (right, down)),
        (packs.at[0, 0:32], side_r.at[32 + PH : ROWS], (left, up)),
        (packs.at[1, 0:32], side_l.at[32 + PH : ROWS], (right, up)),
    )
    halos = [
        pltpu.make_async_remote_copy(
            src_ref=src, dst_ref=dst, send_sem=halo_send.at[i], recv_sem=halo_recv.at[i],
            device_id=target, device_id_type=MESH,
        )
        for i, (src, dst, target) in enumerate(routes)
    ]
    for halo in halos:
        halo.start()
    for halo in halos:
        halo.wait()

    lane_r = iota((ROWS, 128), 1)
    sub_r = iota((ROWS, 128), 0)
    has_up, has_down, has_left, has_right = row > 0, row < 15, col > 0, col < 7
    live = jnp.where(has_up, 0, 32), jnp.where(has_down, ROWS, ROWS - 32)
    inside = (sub_r >= live[0]) & (sub_r < live[1])
    lane_o = iota((PH, 128), 1)

    def convolve(b, _):
        top = jnp.where(has_up, above[b].astype(jnp.float32), 0.0)
        bottom = jnp.where(has_down, below[b].astype(jnp.float32), 0.0)
        full = jnp.concatenate([top, sums[b, :, 0:PW], bottom], axis=0)
        tile0, tile1 = full[:, 0:128], full[:, 128:256]
        back = 128 - b * HALF
        edge_l = pltpu.roll(side_l[...].astype(jnp.float32), (back + 108) & 127, 1)
        edge_r = pltpu.roll(side_r[...].astype(jnp.float32), back & 127, 1)
        edge_l = jnp.where(inside & has_left, edge_l, 0.0)
        edge_r = jnp.where(inside & has_right, edge_r, 0.0)
        windows = (
            jnp.where(lane_r < 108, tile0, edge_l),
            pltpu.roll(jnp.where(lane_r < 32, tile1, tile0), 64, 1),
            jnp.where(lane_r < 108, tile1, tile0),
            pltpu.roll(jnp.where(lane_r < 32, edge_r, tile1), 64, 1),
        )
        for a, window in enumerate(windows):
            image32[b & 1, pl.ds(a, ROWS, stride=4), :] = window
        low = image32[b & 1, 0 : 4 * ROWS].astype(jnp.bfloat16)
        image2[b & 1, :, 0:128] = low
        image2[b & 1, 0 : 4 * ROWS - 16, 128:256] = low[16:]
        left_side = jnp.concatenate(
            [image2[b & 1, 4 * FIRST + 32 * p : 4 * FIRST + 32 * p + OUT_ROWS] for p in range(SHIFTS // 2)], axis=1
        )
        full_prod = lax.dot_general(
            left_side, weights[b], (((1,), (1,)), ((), ())), preferred_element_type=jnp.float32
        )
        prod[b & 1, 0 : OUT_ROWS - 8] = full_prod[0 : OUT_ROWS - 8, 0:128] + full_prod[8:OUT_ROWS, 128:256]
        for h in range(2):
            e0 = prod[b & 1, pl.ds(2 * h, PH, stride=4), :]
            e0n = prod[b & 1, pl.ds(2 * h + 4, PH, stride=4), :]
            e1 = prod[b & 1, pl.ds(2 * h + 1, PH, stride=4), :]
            e1n = prod[b & 1, pl.ds(2 * h + 5, PH, stride=4), :]
            kept = jnp.where(lane_o < TILE, e0, e1n)
            moved = jnp.where(lane_o < TILE, e1, e0n)
            out_v[b, :, h * 128 : (h + 1) * 128] = kept + pltpu.roll(moved, TILE, 1)
        return 0

    for b in range(BANDS):
        convolve(b, 0)
    result = pltpu.make_async_copy(out_v, out_hbm, out_sem)
    result.start()
    result.wait()


def on_device(
    block_pixels,
    block_ivar,
    block_mask,
    block_patch,
    block_offset,
    block_exposure,
    exposure_band,
    basis,
    coefficients,
):
    f32, bf16, i32 = jnp.float32, jnp.bfloat16, jnp.int32
    lines = [v.reshape(1, v.size) for v in (block_patch, block_offset, block_exposure, exposure_band)]
    scales = coefficients.transpose(0, 3, 1, 2)
    vmem, smem, hbm = pltpu.VMEM, pltpu.SMEM, pltpu.HBM
    dma = pltpu.SemaphoreType.DMA
    return pl.pallas_call(
        body,
        out_shape=jax.ShapeDtypeStruct((BANDS, PH, PW), f32),
        in_specs=[pl.BlockSpec(memory_space=hbm)] * 9,
        out_specs=pl.BlockSpec(memory_space=hbm),
        scratch_shapes=[
            vmem((128, BH, PW), f32),
            vmem((128, BH, PW), bf16),
            vmem((128, BH, PW), i32),
            vmem((1, 128), i32),
            vmem((1, 128), i32),
            vmem((1, 128), i32),
            vmem((1, exposure_band.size), i32),
            vmem(basis.shape, f32),
            smem(scales.shape, f32),
            vmem((TAPS, 128), f32),
            vmem((8, 128), i32),
            smem((8, 128), i32),
            vmem((128, 128), i32),
            vmem((128, 128), i32),
            vmem((2048, 2 * PW), bf16),
            vmem((2048, 2 * PW), bf16),
            vmem((BANDS, PH, 2 * PW), f32),
            vmem((BANDS, GROUP * TILE, SHIFTS * 128), bf16),
            vmem((BANDS, PH, PW), bf16),
            vmem((2, PH, 128), bf16),
            vmem((BANDS, 32, PW), bf16),
            vmem((BANDS, 32, PW), bf16),
            vmem((ROWS, 128), bf16),
            vmem((ROWS, 128), bf16),
            vmem((2, 4 * ROWS + 8, 128), f32),
            vmem((2, 4 * ROWS, 256), bf16),
            vmem((2, OUT_ROWS, 128), f32),
            vmem((BANDS, PH, PW), f32),
            dma((9,)),
            dma,
            dma,
            dma((8,)),
            dma,
            dma((8,)),
            dma((8,)),
            dma((8,)),
            dma,
            pltpu.SemaphoreType.REGULAR,
            pltpu.SemaphoreType.REGULAR,
        ],
        compiler_params=pltpu.CompilerParams(
            collective_id=0, has_side_effects=True, vmem_limit_bytes=56 << 20
        ),
        cost_estimate=pl.CostEstimate(flops=6 << 30, bytes_accessed=4 << 20, transcendentals=0),
    )(block_pixels, block_ivar, block_mask, *lines, basis, scales)


def solution(mesh):
    placed = (
        P(("col", "row"), None, None),
        P(("col", "row"), None, None),
        P(("col", "row"), None, None),
        P(("col", "row"), None),
        P(("col", "row")),
        P(("col", "row")),
        P(),
        P(),
        P("row", "col", None, None),
    )
    return jax.shard_map(
        on_device, mesh=mesh, in_specs=placed, out_specs=P(None, "row", "col"), check_vma=False
    )
```

```python
import jax
import jax.numpy as jnp
from jax import lax
from jax.experimental import pallas as pl
from jax.experimental.pallas import tpu as pltpu
from jax.sharding import PartitionSpec as P

BANDS = 6
NBASIS = 5
KS = 41
HALF = 20
PH = 128
PW = 256
BH = 8
MESH = pl.DeviceIdType.MESH

STEP_X = (-2134884224, -1862789622, 1547504322, -997211824, 1521461850, -1521111046, -2790657, 930528599)
STEP_Y = (-1473245152, 621707680, 130240700, 824245269, -1347790166, 1516198495, 2105372591, 904625533)
STEP_Z = (672072970, 1252255834, -246087895, 998725, -84236886, 1437267365, -715665414, 15743)
STEP_C = (285475844, 71372868, 1091585041, 1431572740, 1145324612, 1145324612, 286331972, 357912849)
LINES, PLANES = 13, 64

GROUP = 4
TILE = 64
TAPS = 44
SHIFTS = TAPS // GROUP
ROWS = PH + 64
FIRST = 32 - HALF
OUT_ROWS = 528


def iota(shape, dim):
    return lax.broadcasted_iota(jnp.int32, shape, dim)


def body(
    pix_hbm,
    ivar_hbm,
    mask_hbm,
    patch_hbm,
    offset_hbm,
    exposure_hbm,
    band_hbm,
    basis_hbm,
    coef_hbm,
    out_ref,
    pix,
    ivar,
    mask,
    patch_ref,
    offset_ref,
    exposure_ref,
    band_ref,
    basis_ref,
    coef_ref,
    taps_ref,
    table,
    table_s,
    label,
    label_in,
    data,
    data_in,
    sums,
    weights,
    mean_b,
    packs,
    above,
    below,
    side_l,
    side_r,
    image32,
    image2,
    full,
    prod,
    in_sem,
    table_sem,
    data_send,
    data_recv,
    label_send,
    label_recv,
    halo_send,
    halo_recv,
    line_sem,
    plane_sem,
):
    col = lax.axis_index("col")
    row = lax.axis_index("row")
    me = col * 16 + row
    z, core, x, y = col >> 1, col & 1, row >> 2, row & 3

    loads = [
        pltpu.make_async_copy(src, dst, in_sem.at[i])
        for i, (src, dst) in enumerate(
            (
                (patch_hbm, patch_ref),
                (offset_hbm, offset_ref),
                (exposure_hbm, exposure_ref),
                (band_hbm, band_ref),
                (pix_hbm, pix),
                (ivar_hbm, ivar),
                (mask_hbm, mask),
                (basis_hbm, basis_ref),
                (coef_hbm, coef_ref),
            )
        )
    ]
    barrier = pltpu.get_barrier_semaphore()
    on_line = (
        [((col + d) & 7, row) for d in range(1, 8)]
        + [(col, x * 4 + ((y + d) & 3)) for d in range(1, 4)]
        + [(col, ((x + d) & 3) * 4 + y) for d in range(1, 4)]
    )
    for peer in on_line:
        pl.semaphore_signal(barrier, inc=1, device_id=peer, device_id_type=MESH)
    for load in loads:
        load.start()
    for load in loads[:4]:
        load.wait()

    square = (128, 128)
    sub, lane = iota(square, 0), iota(square, 1)
    diag = sub == lane

    def to_column(line):
        return jnp.sum(jnp.where(diag, line, 0.0), axis=1, keepdims=True)

    def to_line(column):
        return jnp.sum(jnp.where(diag, column, 0.0), axis=0, keepdims=True)

    subf, lanef = sub.astype(jnp.float32), lane.astype(jnp.float32)
    patch = patch_ref[...].astype(jnp.float32)
    exposures = band_ref.shape[1]
    band_line = jnp.broadcast_to(band_ref[...].astype(jnp.float32), (exposures, exposures))
    band_col = jnp.sum(
        jnp.where(iota(band_line.shape, 0) == iota(band_line.shape, 1), band_line, 0.0), axis=1, keepdims=True
    )
    band_line = jnp.sum(
        jnp.where(exposure_ref[...].astype(jnp.float32) == subf[0:exposures], band_col, 0.0), axis=0, keepdims=True
    )
    key_line = band_line * float(PH) + offset_ref[...].astype(jnp.float32)
    named = patch == subf
    low = jnp.min(jnp.where(named, lanef, 128.0), axis=1, keepdims=True)
    high = jnp.max(jnp.where(named, lanef, -1.0), axis=1, keepdims=True)
    key_low = jnp.sum(jnp.where(lanef == low, key_line, 0.0), axis=1, keepdims=True)
    key_high = jnp.sum(jnp.where(lanef == high, key_line, 0.0), axis=1, keepdims=True)
    key_low = jnp.where(low < 128.0, key_low, -1000.0)
    key_high = jnp.where(high > low, key_high, -1000.0)
    place = (lane & 15) < BH
    label[...] = (jnp.where(place, key_low, key_high) + (lane & 7).astype(jnp.float32)).astype(jnp.int32)
    low_line = to_line(jnp.minimum(low, 127.0))
    high_line = to_line(jnp.maximum(high, 0.0))
    table[...] = jnp.where(iota((8, 128), 0) == 0, low_line, high_line).astype(jnp.int32)
    to_smem = pltpu.make_async_copy(table, table_s, table_sem)
    to_smem.start()
    to_smem.wait()

    for load in loads[4:]:
        load.wait()

    def fill(owner, into, at):
        first, second = table_s[0, owner] & 127, table_s[1, owner] & 127
        w0 = mask[first].astype(jnp.float32) * ivar[first].astype(jnp.float32)
        w1 = mask[second].astype(jnp.float32) * ivar[second].astype(jnp.float32)
        p0, p1 = w0 * pix[first], w1 * pix[second]
        into[pl.ds(at, 16), 0:PW] = jnp.concatenate([p0, p1], axis=0).astype(jnp.bfloat16)
        into[pl.ds(at, 16), PW : 2 * PW] = jnp.concatenate([w0, w1], axis=0).astype(jnp.bfloat16)

    def transfer(k, owner, group, target):
        rows = pl.ds(pl.multiple_of(k * 16, 16), 16)
        return (
            pltpu.make_async_remote_copy(
                src_ref=data.at[rows],
                dst_ref=data_in.at[rows],
                send_sem=data_send,
                recv_sem=data_recv.at[group],
                device_id=target,
                device_id_type=MESH,
            ),
            pltpu.make_async_remote_copy(
                src_ref=label.at[pl.ds(owner, 1)],
                dst_ref=label_in.at[pl.ds(k, 1)],
                send_sem=label_send,
                recv_sem=label_recv.at[group],
                device_id=target,
                device_id_type=MESH,
            ),
        )

    def send_some(first, last):
        group = first // 16
        words = [steps[group] for steps in (STEP_X, STEP_Y, STEP_Z, STEP_C)]

        def send(m, _):
            k = group * 16 + m
            dx, dy, dz, dc = [(jnp.int32(word) >> (2 * m)) & 3 for word in words]
            to_col = ((z + dz) & 3) * 2 + (core ^ dc)
            to_row = ((x + dx) & 3) * 4 + ((y + dy) & 3)
            owner = to_col * 16 + to_row
            fill(owner, data, pl.multiple_of(k * 16, 16))
            for copy in transfer(k, owner, group, (to_col, to_row)):
                copy.start()
            return 0

        lax.fori_loop(first - group * 16, last - group * 16, send, 0)

    pl.semaphore_wait(barrier, len(on_line))
    for peer in on_line:
        pl.semaphore_signal(line_sem, inc=1, device_id=peer, device_id_type=MESH)
    send_some(0, LINES)
    pl.semaphore_wait(line_sem, len(on_line))
    for peer in on_line[-3:]:
        pl.semaphore_signal(plane_sem, inc=1, device_id=peer, device_id_type=MESH)
    send_some(LINES, 16)
    for first in range(16, PLANES, 16):
        send_some(first, first + 16)
    pl.semaphore_wait(plane_sem, 3)
    for first in range(PLANES, 128, 16):
        send_some(first, min(first + 16, 127))
    fill(me, data_in, 127 * 16)
    own = pltpu.make_async_copy(label.at[pl.ds(me, 1)], label_in.at[pl.ds(127, 1)], table_sem)
    own.start()
    own.wait()

    taps_ref[...] = jnp.zeros_like(taps_ref)

    def build(b, _):
        combined = coef_ref[0, 0, 0, b] * basis_ref[0]
        for k in range(1, NBASIS):
            combined = combined + coef_ref[0, k, 0, b] * basis_ref[k]
        taps_ref[0:KS, 0:KS] = combined
        taps = taps_ref[...]
        for d in range(TAPS):
            i, s = d // GROUP, d % GROUP
            base = pltpu.roll(jnp.broadcast_to(taps[d : d + 1], (8, 128)), 0, 1, stride=1, stride_axis=0)
            spread = jnp.concatenate(
                [pltpu.roll(base, (128 - HALF + q) % 128, 1) for q in range(0, TILE, 8)], axis=0
            )
            weights[b, s * TILE : (s + 1) * TILE, i * 128 : (i + 1) * 128] = spread.astype(jnp.bfloat16)
        return 0

    lax.fori_loop(0, BANDS, build, 0)

    for group in range(8):
        count = 15 if group == 7 else 16
        big = pl.ds(group * 256, count * 16)
        small = pl.ds(group * 16, count)
        pltpu.make_async_remote_copy(
            src_ref=label.at[small], dst_ref=label_in.at[small], send_sem=label_send,
            recv_sem=label_recv.at[group], device_id=(col ^ 1, row), device_id_type=MESH,
        ).wait_recv()
        pltpu.make_async_remote_copy(
            src_ref=data.at[big], dst_ref=data_in.at[big], send_sem=data_send,
            recv_sem=data_recv.at[group], device_id=(col ^ 1, row), device_id_type=MESH,
        ).wait_recv()
        pick = iota((8, 128), 1) >> 4 == iota((8, 128), 0)
        lines = [
            jnp.sum(
                jnp.where(pick, label_in[group * 16 + h * 8 : group * 16 + h * 8 + 8].astype(jnp.float32), 0.0),
                axis=0,
                keepdims=True,
            )
            for h in range(2)
        ]
        line = jnp.concatenate(lines, axis=1).astype(jnp.int32)
        for b in range(BANDS):
            hit = iota((PH, 256), 0) + b * PH == line
            part = jnp.dot(
                hit.astype(jnp.float32).astype(jnp.bfloat16),
                data_in[group * 256 : (group + 1) * 256],
                preferred_element_type=jnp.float32,
            )
            if group:
                sums[b] += part
            else:
                sums[b] = part

    pltpu.make_async_remote_copy(
        src_ref=data.at[pl.ds(0, 127 * 16)], dst_ref=data_in.at[pl.ds(0, 127 * 16)], send_sem=data_send,
        recv_sem=data_recv.at[0], device_id=(col ^ 1, row), device_id_type=MESH,
    ).wait_send()
    pltpu.make_async_remote_copy(
        src_ref=label.at[pl.ds(0, 127)], dst_ref=label_in.at[pl.ds(0, 127)], send_sem=label_send,
        recv_sem=label_recv.at[0], device_id=(col ^ 1, row), device_id_type=MESH,
    ).wait_send()

    up, down = (row + 15) & 15, (row + 1) & 15
    left, right = (col + 7) & 7, (col + 1) & 7

    def halo(src, dst, i, target):
        return pltpu.make_async_remote_copy(
            src_ref=src, dst_ref=dst, send_sem=halo_send.at[i], recv_sem=halo_recv.at[i],
            device_id=target, device_id_type=MESH,
        )

    lane_p = iota((PH, 128), 1)
    pack_l = jnp.zeros((PH, 128), jnp.float32)
    pack_r = jnp.zeros((PH, 128), jnp.float32)
    for b in range(BANDS):
        mean = sums[b, :, 0:PW] / jnp.maximum(sums[b, :, PW : 2 * PW], 1.0)
        sums[b, :, 0:PW] = mean
        mean_b[b] = mean.astype(jnp.bfloat16)
        halo(mean_b.at[b, PH - 32 : PH], above.at[b], 0, (col, down)).start()
        halo(mean_b.at[b, 0:32], below.at[b], 1, (col, up)).start()
        here = (lane_p >= b * HALF) & (lane_p < (b + 1) * HALF)
        pack_l = jnp.where(here, pltpu.roll(mean[:, 0:128], b * HALF, 1), pack_l)
        pack_r = jnp.where(here, pltpu.roll(mean[:, 128:256], (b * HALF + HALF) % 128, 1), pack_r)
    packs[0] = pack_l.astype(jnp.bfloat16)
    packs[1] = pack_r.astype(jnp.bfloat16)
    sides = [
        halo(packs.at[0], side_r.at[32 : 32 + PH], 2, (left, row)),
        halo(packs.at[1], side_l.at[32 : 32 + PH], 3, (right, row)),
    ]
    corners = [
        halo(packs.at[0, PH - 32 : PH], side_r.at[0:32], 4, (left, down)),
        halo(packs.at[1, PH - 32 : PH], side_l.at[0:32], 5, (right, down)),
        halo(packs.at[0, 0:32], side_r.at[32 + PH : ROWS], 6, (left, up)),
        halo(packs.at[1, 0:32], side_l.at[32 + PH : ROWS], 7, (right, up)),
    ]
    for copy in sides + corners:
        copy.start()

    has_up, has_down, has_left, has_right = row > 0, row < 15, col > 0, col < 7

    def inner_windows(b, tile0, tile1, first):
        rows = tile0.shape[0]
        lanes = iota((rows, 128), 1)
        image32[b, pl.ds(4 * first + 1, rows, stride=4), :] = pltpu.roll(jnp.where(lanes < 32, tile1, tile0), 64, 1)
        image32[b, pl.ds(4 * first + 2, rows, stride=4), :] = jnp.where(lanes < 108, tile1, tile0)

    def outer_windows(b, tile0, tile1, edge_l, edge_r, first):
        rows = tile0.shape[0]
        lanes = iota((rows, 128), 1)
        edge_l = jnp.where(has_left, pltpu.roll(edge_l.astype(jnp.float32), (236 - b * HALF) % 128, 1), 0.0)
        edge_r = jnp.where(has_right, pltpu.roll(edge_r.astype(jnp.float32), (128 - b * HALF) % 128, 1), 0.0)
        image32[b, pl.ds(4 * first, rows, stride=4), :] = jnp.where(lanes < 108, tile0, edge_l)
        image32[b, pl.ds(4 * first + 3, rows, stride=4), :] = pltpu.roll(jnp.where(lanes < 32, edge_r, tile1), 64, 1)

    def widen(b, first, last, first2, last2):
        image2[b, first:last, 0:128] = image32[b, first:last].astype(jnp.bfloat16)
        image2[b, first2:last2, 128:256] = image32[b, first2 + 16 : last2 + 16].astype(jnp.bfloat16)

    def matmul(b, spans):
        pairs = [
            jnp.concatenate(
                [image2[b, 4 * FIRST + 32 * p + lo : 4 * FIRST + 32 * p + hi] for lo, hi in spans], axis=0
            )
            for p in range(SHIFTS // 2)
        ]
        if SHIFTS % 2:
            pairs.append(
                jnp.concatenate(
                    [
                        image2[b, 4 * FIRST + 16 * (SHIFTS - 1) + lo : 4 * FIRST + 16 * (SHIFTS - 1) + hi, 0:128]
                        for lo, hi in spans
                    ],
                    axis=0,
                )
            )
        result = lax.dot_general(
            jnp.concatenate(pairs, axis=1), weights[b], (((1,), (1,)), ((), ())), preferred_element_type=jnp.float32
        )
        at = 0
        for lo, hi in spans:
            full[b, lo:hi] = result[at : at + hi - lo]
            at += hi - lo

    def finish(b, lo, hi):
        first, last = 4 * lo, 4 * hi + 8
        prod[b, first:last] = full[b, first:last, 0:128] + full[b, first + 8 : last + 8, 128:256]
        rows = hi - lo
        lanes = iota((rows, 128), 1)
        for h in range(2):
            e0, e0n, e1, e1n = [prod[b, pl.ds(first + 2 * h + i, rows, stride=4), :] for i in (0, 4, 1, 5)]
            kept = jnp.where(lanes < TILE, e0, e1n)
            moved = jnp.where(lanes < TILE, e1, e0n)
            out_ref[b, lo:hi, h * 128 : (h + 1) * 128] = kept + pltpu.roll(moved, TILE, 1)

    for b in range(BANDS):
        inner_windows(b, sums[b, :, 0:128], sums[b, :, 128:256], 32)
    for copy in sides:
        copy.wait()
    for b in range(BANDS):
        outer_windows(
            b, sums[b, :, 0:128], sums[b, :, 128:256], side_l[32 : 32 + PH], side_r[32 : 32 + PH], 32
        )
        widen(b, 128, 640, 128, 608)
        matmul(b, ((80, 432),))
        finish(b, 24, 104)

    for copy in corners:
        copy.wait()
    halo(mean_b.at[:, PH - 32 : PH], above, 0, (col, down)).wait()
    halo(mean_b.at[:, 0:32], below, 1, (col, up)).wait()
    for b in range(BANDS):
        for ref, here, first, side in ((above, has_up, 0, 0), (below, has_down, 32 + PH, 32 + PH)):
            rows = jnp.where(here, ref[b].astype(jnp.float32), 0.0)
            edge_l = jnp.where(here, side_l[side : side + 32].astype(jnp.float32), 0.0)
            edge_r = jnp.where(here, side_r[side : side + 32].astype(jnp.float32), 0.0)
            inner_windows(b, rows[:, 0:128], rows[:, 128:256], first)
            outer_windows(b, rows[:, 0:128], rows[:, 128:256], edge_l, edge_r, first)
        widen(b, 48, 128, 48, 128)
        widen(b, 640, 736, 608, 736)
        matmul(b, ((0, 80), (432, OUT_ROWS)))
        finish(b, 0, 24)
        finish(b, 104, 128)


def on_device(
    block_pixels,
    block_ivar,
    block_mask,
    block_patch,
    block_offset,
    block_exposure,
    exposure_band,
    basis,
    coefficients,
):
    f32, bf16, i32 = jnp.float32, jnp.bfloat16, jnp.int32
    lines = [v.reshape(1, v.size) for v in (block_patch, block_offset, block_exposure, exposure_band)]
    scales = coefficients.transpose(0, 3, 1, 2)
    vmem, smem, hbm = pltpu.VMEM, pltpu.SMEM, pltpu.HBM
    dma = pltpu.SemaphoreType.DMA
    return pl.pallas_call(
        body,
        out_shape=vmem((BANDS, PH, PW), f32),
        in_specs=[pl.BlockSpec(memory_space=hbm)] * 9,
        out_specs=pl.BlockSpec(memory_space=vmem),
        scratch_shapes=[
            vmem((128, BH, PW), f32),
            vmem((128, BH, PW), bf16),
            vmem((128, BH, PW), i32),
            vmem((1, 128), i32),
            vmem((1, 128), i32),
            vmem((1, 128), i32),
            vmem((1, exposure_band.size), i32),
            vmem(basis.shape, f32),
            smem(scales.shape, f32),
            vmem((TAPS, 128), f32),
            vmem((8, 128), i32),
            smem((8, 128), i32),
            vmem((128, 128), i32),
            vmem((128, 128), i32),
            vmem((2048, 2 * PW), bf16),
            vmem((2048, 2 * PW), bf16),
            vmem((BANDS, PH, 2 * PW), f32),
            vmem((BANDS, GROUP * TILE, SHIFTS * 128), bf16),
            vmem((BANDS, PH, PW), bf16),
            vmem((2, PH, 128), bf16),
            vmem((BANDS, 32, PW), bf16),
            vmem((BANDS, 32, PW), bf16),
            vmem((ROWS, 128), bf16),
            vmem((ROWS, 128), bf16),
            vmem((BANDS, 4 * ROWS + 8, 128), f32),
            vmem((BANDS, 4 * ROWS, 256), bf16),
            vmem((BANDS, OUT_ROWS, 256), f32),
            vmem((BANDS, OUT_ROWS, 128), f32),
            dma((9,)),
            dma,
            dma,
            dma((8,)),
            dma,
            dma((8,)),
            dma((8,)),
            dma((8,)),
            pltpu.SemaphoreType.REGULAR,
            pltpu.SemaphoreType.REGULAR,
        ],
        compiler_params=pltpu.CompilerParams(
            collective_id=0, has_side_effects=True, vmem_limit_bytes=56 << 20
        ),
        cost_estimate=pl.CostEstimate(flops=6 << 30, bytes_accessed=4 << 20, transcendentals=0),
    )(block_pixels, block_ivar, block_mask, *lines, basis, scales)


def solution(mesh):
    placed = (
        P(("col", "row"), None, None),
        P(("col", "row"), None, None),
        P(("col", "row"), None, None),
        P(("col", "row"), None),
        P(("col", "row")),
        P(("col", "row")),
        P(),
        P(),
        P("row", "col", None, None),
    )
    return jax.shard_map(
        on_device, mesh=mesh, in_specs=placed, out_specs=P(None, "row", "col"), check_vma=False
    )
```

```python
import jax
import jax.numpy as jnp
from jax import lax
from jax.experimental import pallas as pl
from jax.experimental.pallas import tpu as pltpu
from jax.sharding import PartitionSpec as P

BANDS = 6
NBASIS = 5
KS = 41
HALF = 20
PH = 128
PW = 256
BH = 8
MESH = pl.DeviceIdType.MESH

STEP_X = (-2134884224, -1862789622, 1547504322, -997211824, 1521461850, -1521111046, -2790657, 930528599)
STEP_Y = (-1473245152, 621707680, 130240700, 824245269, -1347790166, 1516198495, 2105372591, 904625533)
STEP_Z = (672072970, 1252255834, -246087895, 998725, -84236886, 1437267365, -715665414, 15743)
STEP_C = (285475844, 71372868, 1091585041, 1431572740, 1145324612, 1145324612, 286331972, 357912849)
LINES, PLANES = 13, 64

GROUP = 4
TILE = 64
TAPS = 44
SHIFTS = TAPS // GROUP
ROWS = PH + 64
FIRST = 32 - HALF
OUT_ROWS = 528
LAST = 4 * (32 + PH + HALF)


def iota(shape, dim):
    return lax.broadcasted_iota(jnp.int32, shape, dim)


def body(
    pix_hbm,
    ivar_hbm,
    mask_hbm,
    patch_hbm,
    offset_hbm,
    exposure_hbm,
    band_hbm,
    basis_hbm,
    coef_hbm,
    out_ref,
    pix,
    ivar,
    mask,
    patch_ref,
    offset_ref,
    exposure_ref,
    band_ref,
    basis_ref,
    coef_ref,
    taps_ref,
    table,
    table_s,
    label,
    label_in,
    data,
    data_in,
    sums,
    weights,
    ends,
    ends_b,
    packs,
    above,
    below,
    side_l,
    side_r,
    corner,
    image32,
    image2,
    full,
    prod,
    in_sem,
    table_sem,
    data_send,
    data_recv,
    label_send,
    label_recv,
    halo_send,
    halo_recv,
    line_sem,
    plane_sem,
):
    col = lax.axis_index("col")
    row = lax.axis_index("row")
    me = col * 16 + row
    z, core, x, y = col >> 1, col & 1, row >> 2, row & 3

    loads = [
        pltpu.make_async_copy(src, dst, in_sem.at[i])
        for i, (src, dst) in enumerate(
            (
                (patch_hbm, patch_ref),
                (offset_hbm, offset_ref),
                (exposure_hbm, exposure_ref),
                (band_hbm, band_ref),
                (pix_hbm, pix),
                (ivar_hbm, ivar),
                (mask_hbm, mask),
                (basis_hbm, basis_ref),
                (coef_hbm, coef_ref),
            )
        )
    ]
    barrier = pltpu.get_barrier_semaphore()
    on_line = (
        [((col + d) & 7, row) for d in range(1, 8)]
        + [(col, x * 4 + ((y + d) & 3)) for d in range(1, 4)]
        + [(col, ((x + d) & 3) * 4 + y) for d in range(1, 4)]
    )
    for peer in on_line:
        pl.semaphore_signal(barrier, inc=1, device_id=peer, device_id_type=MESH)
    for load in loads:
        load.start()
    for load in loads[:4]:
        load.wait()

    square = (128, 128)
    sub, lane = iota(square, 0), iota(square, 1)
    diag = sub == lane

    def to_column(line):
        return jnp.sum(jnp.where(diag, line, 0.0), axis=1, keepdims=True)

    def to_line(column):
        return jnp.sum(jnp.where(diag, column, 0.0), axis=0, keepdims=True)

    subf, lanef = sub.astype(jnp.float32), lane.astype(jnp.float32)
    patch = patch_ref[...].astype(jnp.float32)
    exposures = band_ref.shape[1]
    band_line = jnp.broadcast_to(band_ref[...].astype(jnp.float32), (exposures, exposures))
    band_col = jnp.sum(
        jnp.where(iota(band_line.shape, 0) == iota(band_line.shape, 1), band_line, 0.0), axis=1, keepdims=True
    )
    band_line = jnp.sum(
        jnp.where(exposure_ref[...].astype(jnp.float32) == subf[0:exposures], band_col, 0.0), axis=0, keepdims=True
    )
    key_line = band_line * float(PH) + offset_ref[...].astype(jnp.float32)
    named = patch == subf
    low = jnp.min(jnp.where(named, lanef, 128.0), axis=1, keepdims=True)
    high = jnp.max(jnp.where(named, lanef, -1.0), axis=1, keepdims=True)
    key_low = jnp.sum(jnp.where(lanef == low, key_line, 0.0), axis=1, keepdims=True)
    key_high = jnp.sum(jnp.where(lanef == high, key_line, 0.0), axis=1, keepdims=True)
    key_low = jnp.where(low < 128.0, key_low, -1000.0)
    key_high = jnp.where(high > low, key_high, -1000.0)
    place = (lane & 15) < BH
    label[...] = (jnp.where(place, key_low, key_high) + (lane & 7).astype(jnp.float32)).astype(jnp.int32)
    low_line = to_line(jnp.minimum(low, 127.0))
    high_line = to_line(jnp.maximum(high, 0.0))
    table[...] = jnp.where(iota((8, 128), 0) == 0, low_line, high_line).astype(jnp.int32)
    to_smem = pltpu.make_async_copy(table, table_s, table_sem)
    to_smem.start()
    to_smem.wait()

    for load in loads[4:]:
        load.wait()

    def fill(owner, into, at):
        first, second = table_s[0, owner] & 127, table_s[1, owner] & 127
        w0 = mask[first].astype(jnp.float32) * ivar[first].astype(jnp.float32)
        w1 = mask[second].astype(jnp.float32) * ivar[second].astype(jnp.float32)
        p0, p1 = w0 * pix[first], w1 * pix[second]
        into[pl.ds(at, 16), 0:PW] = jnp.concatenate([p0, p1], axis=0).astype(jnp.bfloat16)
        into[pl.ds(at, 16), PW : 2 * PW] = jnp.concatenate([w0, w1], axis=0).astype(jnp.bfloat16)

    def transfer(k, owner, group, target):
        rows = pl.ds(pl.multiple_of(k * 16, 16), 16)
        return (
            pltpu.make_async_remote_copy(
                src_ref=data.at[rows],
                dst_ref=data_in.at[rows],
                send_sem=data_send,
                recv_sem=data_recv.at[group],
                device_id=target,
                device_id_type=MESH,
            ),
            pltpu.make_async_remote_copy(
                src_ref=label.at[pl.ds(owner, 1)],
                dst_ref=label_in.at[pl.ds(k, 1)],
                send_sem=label_send,
                recv_sem=label_recv.at[group],
                device_id=target,
                device_id_type=MESH,
            ),
        )

    def send_some(first, last):
        group = first // 16
        words = [steps[group] for steps in (STEP_X, STEP_Y, STEP_Z, STEP_C)]

        def send(m, _):
            k = group * 16 + m
            dx, dy, dz, dc = [(jnp.int32(word) >> (2 * m)) & 3 for word in words]
            to_col = ((z + dz) & 3) * 2 + (core ^ dc)
            to_row = ((x + dx) & 3) * 4 + ((y + dy) & 3)
            owner = to_col * 16 + to_row
            fill(owner, data, pl.multiple_of(k * 16, 16))
            for copy in transfer(k, owner, group, (to_col, to_row)):
                copy.start()
            return 0

        lax.fori_loop(first - group * 16, last - group * 16, send, 0)

    pl.semaphore_wait(barrier, len(on_line))
    for peer in on_line:
        pl.semaphore_signal(line_sem, inc=1, device_id=peer, device_id_type=MESH)
    send_some(0, LINES)
    pl.semaphore_wait(line_sem, len(on_line))
    for peer in on_line[-3:]:
        pl.semaphore_signal(plane_sem, inc=1, device_id=peer, device_id_type=MESH)
    send_some(LINES, 16)
    for first in range(16, PLANES, 16):
        send_some(first, first + 16)
    pl.semaphore_wait(plane_sem, 3)
    for first in range(PLANES, 128, 16):
        send_some(first, min(first + 16, 127))
    fill(me, data_in, 127 * 16)
    own = pltpu.make_async_copy(label.at[pl.ds(me, 1)], label_in.at[pl.ds(127, 1)], table_sem)
    own.start()
    own.wait()

    taps_ref[...] = jnp.zeros_like(taps_ref)

    def build(b, _):
        combined = coef_ref[0, 0, 0, b] * basis_ref[0]
        for k in range(1, NBASIS):
            combined = combined + coef_ref[0, k, 0, b] * basis_ref[k]
        taps_ref[0:KS, 0:KS] = combined
        taps = taps_ref[...]
        for d in range(TAPS):
            i, s = d // GROUP, d % GROUP
            base = pltpu.roll(jnp.broadcast_to(taps[d : d + 1], (8, 128)), 0, 1, stride=1, stride_axis=0)
            spread = jnp.concatenate(
                [pltpu.roll(base, (128 - HALF + q) % 128, 1) for q in range(0, TILE, 8)], axis=0
            )
            weights[b, s * TILE : (s + 1) * TILE, i * 128 : (i + 1) * 128] = spread.astype(jnp.bfloat16)
        return 0

    lax.fori_loop(0, BANDS, build, 0)

    for group in range(8):
        count = 15 if group == 7 else 16
        big = pl.ds(group * 256, count * 16)
        small = pl.ds(group * 16, count)
        pltpu.make_async_remote_copy(
            src_ref=label.at[small], dst_ref=label_in.at[small], send_sem=label_send,
            recv_sem=label_recv.at[group], device_id=(col ^ 1, row), device_id_type=MESH,
        ).wait_recv()
        pltpu.make_async_remote_copy(
            src_ref=data.at[big], dst_ref=data_in.at[big], send_sem=data_send,
            recv_sem=data_recv.at[group], device_id=(col ^ 1, row), device_id_type=MESH,
        ).wait_recv()
        pick = iota((8, 128), 1) >> 4 == iota((8, 128), 0)
        lines = [
            jnp.sum(
                jnp.where(pick, label_in[group * 16 + h * 8 : group * 16 + h * 8 + 8].astype(jnp.float32), 0.0),
                axis=0,
                keepdims=True,
            )
            for h in range(2)
        ]
        line = jnp.concatenate(lines, axis=1).astype(jnp.int32)
        for b in range(BANDS):
            hit = iota((PH, 256), 0) + b * PH == line
            part = jnp.dot(
                hit.astype(jnp.float32).astype(jnp.bfloat16),
                data_in[group * 256 : (group + 1) * 256],
                preferred_element_type=jnp.float32,
            )
            if group:
                sums[b] += part
            else:
                sums[b] = part

    up, down = (row + 15) & 15, (row + 1) & 15
    left, right = (col + 7) & 7, (col + 1) & 7

    def halo(src, dst, i, target):
        return pltpu.make_async_remote_copy(
            src_ref=src, dst_ref=dst, send_sem=halo_send.at[i], recv_sem=halo_recv.at[i],
            device_id=target, device_id_type=MESH,
        )

    lane_p = iota((PH, 128), 1)
    pack_l = jnp.zeros((PH, 128), jnp.float32)
    pack_r = jnp.zeros((PH, 128), jnp.float32)
    for b in range(BANDS):
        mean = sums[b, :, 0:PW] / jnp.maximum(sums[b, :, PW : 2 * PW], 1.0)
        sums[b, :, 0:PW] = mean
        ends[0, b * HALF : (b + 1) * HALF] = mean[PH - HALF : PH]
        ends[1, b * HALF : (b + 1) * HALF] = mean[0:HALF]
        here = (lane_p >= b * HALF) & (lane_p < (b + 1) * HALF)
        pack_l = jnp.where(here, pltpu.roll(mean[:, 0:128], b * HALF, 1), pack_l)
        pack_r = jnp.where(here, pltpu.roll(mean[:, 128:256], (b * HALF + HALF) % 128, 1), pack_r)
    packs[0] = pack_l.astype(jnp.bfloat16)
    packs[1] = pack_r.astype(jnp.bfloat16)
    sides = [
        halo(packs.at[0], side_r.at[32 : 32 + PH], 2, (left, row)),
        halo(packs.at[1], side_l.at[32 : 32 + PH], 3, (right, row)),
    ]
    corners = [
        halo(packs.at[0, PH - 32 : PH], side_r.at[0:32], 4, (left, down)),
        halo(packs.at[1, PH - 32 : PH], side_l.at[0:32], 5, (right, down)),
        halo(packs.at[0, 0:32], side_r.at[32 + PH : ROWS], 6, (left, up)),
        halo(packs.at[1, 0:32], side_l.at[32 + PH : ROWS], 7, (right, up)),
    ]
    for copy in corners + sides:
        copy.start()
    ends[:, BANDS * HALF :] = jnp.zeros_like(ends[:, BANDS * HALF :])
    ends_b[...] = ends[...].astype(jnp.bfloat16)
    rows = [halo(ends_b.at[0], above, 0, (col, down)), halo(ends_b.at[1], below, 1, (col, up))]
    for copy in rows:
        copy.start()

    has_up, has_down, has_left, has_right = row > 0, row < 15, col > 0, col < 7

    def inner_windows(b, tile0, tile1, first):
        rows = tile0.shape[0]
        lanes = iota((rows, 128), 1)
        image32[b, pl.ds(4 * first + 1, rows, stride=4), :] = pltpu.roll(jnp.where(lanes < 32, tile1, tile0), 64, 1)
        image32[b, pl.ds(4 * first + 2, rows, stride=4), :] = jnp.where(lanes < 108, tile1, tile0)

    def outer_windows(b, tile0, tile1, edge_l, edge_r, first):
        rows = tile0.shape[0]
        lanes = iota((rows, 128), 1)
        edge_l = jnp.where(has_left, pltpu.roll(edge_l.astype(jnp.float32), (236 - b * HALF) % 128, 1), 0.0)
        edge_r = jnp.where(has_right, pltpu.roll(edge_r.astype(jnp.float32), (128 - b * HALF) % 128, 1), 0.0)
        image32[b, pl.ds(4 * first, rows, stride=4), :] = jnp.where(lanes < 108, tile0, edge_l)
        image32[b, pl.ds(4 * first + 3, rows, stride=4), :] = pltpu.roll(jnp.where(lanes < 32, edge_r, tile1), 64, 1)

    def widen(b, first, last, first2, last2):
        image2[b, first:last, 0:128] = image32[b, first:last].astype(jnp.bfloat16)
        image2[b, first2:last2, 128:256] = image32[b, first2 + 16 : last2 + 16].astype(jnp.bfloat16)

    def matmul(b, spans):
        pairs = [
            jnp.concatenate(
                [image2[b, 4 * FIRST + 32 * p + lo : 4 * FIRST + 32 * p + hi] for lo, hi in spans], axis=0
            )
            for p in range(SHIFTS // 2)
        ]
        if SHIFTS % 2:
            pairs.append(
                jnp.concatenate(
                    [
                        image2[b, 4 * FIRST + 16 * (SHIFTS - 1) + lo : 4 * FIRST + 16 * (SHIFTS - 1) + hi, 0:128]
                        for lo, hi in spans
                    ],
                    axis=0,
                )
            )
        result = lax.dot_general(
            jnp.concatenate(pairs, axis=1), weights[b], (((1,), (1,)), ((), ())), preferred_element_type=jnp.float32
        )
        at = 0
        for lo, hi in spans:
            full[b, lo:hi] = result[at : at + hi - lo]
            at += hi - lo

    def finish(b, lo, hi):
        first, last = 4 * lo, 4 * hi + 8
        prod[b, first:last] = full[b, first:last, 0:128] + full[b, first + 8 : last + 8, 128:256]
        rows = hi - lo
        lanes = iota((rows, 128), 1)
        for h in range(2):
            e0, e0n, e1, e1n = [prod[b, pl.ds(first + 2 * h + i, rows, stride=4), :] for i in (0, 4, 1, 5)]
            kept = jnp.where(lanes < TILE, e0, e1n)
            moved = jnp.where(lanes < TILE, e1, e0n)
            out_ref[b, lo:hi, h * 128 : (h + 1) * 128] = kept + pltpu.roll(moved, TILE, 1)

    for b in range(BANDS):
        inner_windows(b, sums[b, :, 0:128], sums[b, :, 128:256], 32)
        image32[b, LAST : LAST + 32] = jnp.zeros((32, 128), jnp.float32)
    for copy in sides:
        copy.wait_recv()
    for b in range(BANDS):
        outer_windows(
            b, sums[b, :, 0:128], sums[b, :, 128:256], side_l[32 : 32 + PH], side_r[32 : 32 + PH], 32
        )
        widen(b, 128, 640, 128, 608)
        matmul(b, ((80, 432),))
        finish(b, 24, 104)

    for copy in rows:
        copy.wait_recv()
    strips = ((0, 32 - HALF, 32 - HALF), (1, 0, 32 + PH))
    ends[0] = jnp.where(has_up, above[...].astype(jnp.float32), 0.0)
    ends[1] = jnp.where(has_down, below[...].astype(jnp.float32), 0.0)
    for b in range(BANDS):
        for i, _, first in strips:
            strip = ends[i, b * HALF : (b + 1) * HALF]
            inner_windows(b, strip[:, 0:128], strip[:, 128:256], first)
    for copy in corners:
        copy.wait_recv()
    for i, here, first in ((0, has_up, 0), (1, has_down, 32 + PH)):
        corner[i, 0] = jnp.where(here, side_l[first : first + 32].astype(jnp.float32), 0.0)
        corner[i, 1] = jnp.where(here, side_r[first : first + 32].astype(jnp.float32), 0.0)
    for b in range(BANDS):
        for i, at, first in strips:
            strip = ends[i, b * HALF : (b + 1) * HALF]
            outer_windows(
                b, strip[:, 0:128], strip[:, 128:256], corner[i, 0, at : at + HALF], corner[i, 1, at : at + HALF], first
            )
        widen(b, 48, 128, 48, 128)
        widen(b, 640, 736, 608, 736)
        matmul(b, ((0, 80), (432, OUT_ROWS)))
        finish(b, 0, 24)
        finish(b, 104, 128)

    for copy in sides + rows + corners:
        copy.wait_send()
    pltpu.make_async_remote_copy(
        src_ref=data.at[pl.ds(0, 127 * 16)], dst_ref=data_in.at[pl.ds(0, 127 * 16)], send_sem=data_send,
        recv_sem=data_recv.at[0], device_id=(col ^ 1, row), device_id_type=MESH,
    ).wait_send()
    pltpu.make_async_remote_copy(
        src_ref=label.at[pl.ds(0, 127)], dst_ref=label_in.at[pl.ds(0, 127)], send_sem=label_send,
        recv_sem=label_recv.at[0], device_id=(col ^ 1, row), device_id_type=MESH,
    ).wait_send()


def on_device(
    block_pixels,
    block_ivar,
    block_mask,
    block_patch,
    block_offset,
    block_exposure,
    exposure_band,
    basis,
    coefficients,
):
    f32, bf16, i32 = jnp.float32, jnp.bfloat16, jnp.int32
    lines = [v.reshape(1, v.size) for v in (block_patch, block_offset, block_exposure, exposure_band)]
    scales = coefficients.transpose(0, 3, 1, 2)
    vmem, smem, hbm = pltpu.VMEM, pltpu.SMEM, pltpu.HBM
    dma = pltpu.SemaphoreType.DMA
    return pl.pallas_call(
        body,
        out_shape=vmem((BANDS, PH, PW), f32),
        in_specs=[pl.BlockSpec(memory_space=hbm)] * 9,
        out_specs=pl.BlockSpec(memory_space=vmem),
        scratch_shapes=[
            vmem((128, BH, PW), f32),
            vmem((128, BH, PW), bf16),
            vmem((128, BH, PW), i32),
            vmem((1, 128), i32),
            vmem((1, 128), i32),
            vmem((1, 128), i32),
            vmem((1, exposure_band.size), i32),
            vmem(basis.shape, f32),
            smem(scales.shape, f32),
            vmem((TAPS, 128), f32),
            vmem((8, 128), i32),
            smem((8, 128), i32),
            vmem((128, 128), i32),
            vmem((128, 128), i32),
            vmem((2048, 2 * PW), bf16),
            vmem((2048, 2 * PW), bf16),
            vmem((BANDS, PH, 2 * PW), f32),
            vmem((BANDS, GROUP * TILE, SHIFTS * 128), bf16),
            vmem((2, 128, PW), f32),
            vmem((2, 128, PW), bf16),
            vmem((2, PH, 128), bf16),
            vmem((128, PW), bf16),
            vmem((128, PW), bf16),
            vmem((ROWS, 128), bf16),
            vmem((ROWS, 128), bf16),
            vmem((2, 2, 32, 128), f32),
            vmem((BANDS, 4 * ROWS + 8, 128), f32),
            vmem((BANDS, 4 * ROWS, 256), bf16),
            vmem((BANDS, OUT_ROWS, 256), f32),
            vmem((BANDS, OUT_ROWS, 128), f32),
            dma((9,)),
            dma,
            dma,
            dma((8,)),
            dma,
            dma((8,)),
            dma((8,)),
            dma((8,)),
            pltpu.SemaphoreType.REGULAR,
            pltpu.SemaphoreType.REGULAR,
        ],
        compiler_params=pltpu.CompilerParams(
            collective_id=0, has_side_effects=True, vmem_limit_bytes=56 << 20
        ),
        cost_estimate=pl.CostEstimate(flops=6 << 30, bytes_accessed=4 << 20, transcendentals=0),
    )(block_pixels, block_ivar, block_mask, *lines, basis, scales)


def solution(mesh):
    placed = (
        P(("col", "row"), None, None),
        P(("col", "row"), None, None),
        P(("col", "row"), None, None),
        P(("col", "row"), None),
        P(("col", "row")),
        P(("col", "row")),
        P(),
        P(),
        P("row", "col", None, None),
    )
    return jax.shard_map(
        on_device, mesh=mesh, in_specs=placed, out_specs=P(None, "row", "col"), check_vma=False
    )
```

```python
import jax
import jax.numpy as jnp
from jax import lax
from jax.experimental import pallas as pl
from jax.experimental.pallas import tpu as pltpu
from jax.sharding import PartitionSpec as P

BANDS = 6
NBASIS = 5
KS = 41
HALF = 20
PH = 128
PW = 256
BH = 8
MESH = pl.DeviceIdType.MESH

STEP_X = (-1610415072, 884100632, -1941376697, -997440312, -1782682714, -373949073, 1810198426, 930526717)
STEP_Y = (671138056, -852716666, 304233553, 824382227, 1734851178, -1699252357, 1859770862, 904623991)
STEP_Z = (-1999097790, 1405692129, 1805307164, 1006974, 1524231834, -1497901570, -812206469, 14293)
STEP_C = (22282240, 0, 1431633920, 1431655765, 0, 1430257664, 1431655765, 357913941)
LINES, PLANES = 13, 64

GROUP = 4
TILE = 64
TAPS = 44
SHIFTS = TAPS // GROUP
ROWS = PH + 64
FIRST = 32 - HALF
OUT_ROWS = 528
LAST = 4 * (32 + PH + HALF)


def iota(shape, dim):
    return lax.broadcasted_iota(jnp.int32, shape, dim)


def body(
    pix_hbm,
    ivar_hbm,
    mask_hbm,
    patch_hbm,
    offset_hbm,
    exposure_hbm,
    band_hbm,
    basis_hbm,
    coef_hbm,
    out_ref,
    pix,
    ivar,
    mask,
    patch_ref,
    offset_ref,
    exposure_ref,
    band_ref,
    basis_ref,
    coef_ref,
    taps_ref,
    table,
    table_s,
    label,
    label_in,
    data,
    data_in,
    sums,
    weights,
    ends,
    ends_b,
    packs,
    above,
    below,
    side_l,
    side_r,
    corner,
    image32,
    image2,
    full,
    prod,
    in_sem,
    table_sem,
    data_send,
    data_recv,
    label_send,
    label_recv,
    halo_send,
    halo_recv,
    line_sem,
    plane_sem,
):
    col = lax.axis_index("col")
    row = lax.axis_index("row")
    me = col * 16 + row
    z, core, x, y = col >> 1, col & 1, row >> 2, row & 3

    loads = [
        pltpu.make_async_copy(src, dst, in_sem.at[i])
        for i, (src, dst) in enumerate(
            (
                (patch_hbm, patch_ref),
                (offset_hbm, offset_ref),
                (exposure_hbm, exposure_ref),
                (band_hbm, band_ref),
                (pix_hbm, pix),
                (ivar_hbm, ivar),
                (mask_hbm, mask),
                (basis_hbm, basis_ref),
                (coef_hbm, coef_ref),
            )
        )
    ]
    barrier = pltpu.get_barrier_semaphore()
    on_line = (
        [((col + d) & 7, row) for d in range(1, 8)]
        + [(col, x * 4 + ((y + d) & 3)) for d in range(1, 4)]
        + [(col, ((x + d) & 3) * 4 + y) for d in range(1, 4)]
    )
    for peer in on_line:
        pl.semaphore_signal(barrier, inc=1, device_id=peer, device_id_type=MESH)
    for load in loads:
        load.start()
    for load in loads[:4]:
        load.wait()

    square = (128, 128)
    sub, lane = iota(square, 0), iota(square, 1)
    diag = sub == lane

    def to_column(line):
        return jnp.sum(jnp.where(diag, line, 0.0), axis=1, keepdims=True)

    def to_line(column):
        return jnp.sum(jnp.where(diag, column, 0.0), axis=0, keepdims=True)

    subf, lanef = sub.astype(jnp.float32), lane.astype(jnp.float32)
    patch = patch_ref[...].astype(jnp.float32)
    exposures = band_ref.shape[1]
    band_line = jnp.broadcast_to(band_ref[...].astype(jnp.float32), (exposures, exposures))
    band_col = jnp.sum(
        jnp.where(iota(band_line.shape, 0) == iota(band_line.shape, 1), band_line, 0.0), axis=1, keepdims=True
    )
    band_line = jnp.sum(
        jnp.where(exposure_ref[...].astype(jnp.float32) == subf[0:exposures], band_col, 0.0), axis=0, keepdims=True
    )
    key_line = band_line * float(PH) + offset_ref[...].astype(jnp.float32)
    named = patch == subf
    low = jnp.min(jnp.where(named, lanef, 128.0), axis=1, keepdims=True)
    high = jnp.max(jnp.where(named, lanef, -1.0), axis=1, keepdims=True)
    key_low = jnp.sum(jnp.where(lanef == low, key_line, 0.0), axis=1, keepdims=True)
    key_high = jnp.sum(jnp.where(lanef == high, key_line, 0.0), axis=1, keepdims=True)
    key_low = jnp.where(low < 128.0, key_low, -1000.0)
    key_high = jnp.where(high > low, key_high, -1000.0)
    place = (lane & 15) < BH
    label[...] = (jnp.where(place, key_low, key_high) + (lane & 7).astype(jnp.float32)).astype(jnp.int32)
    low_line = to_line(jnp.minimum(low, 127.0))
    high_line = to_line(jnp.maximum(high, 0.0))
    table[...] = jnp.where(iota((8, 128), 0) == 0, low_line, high_line).astype(jnp.int32)
    to_smem = pltpu.make_async_copy(table, table_s, table_sem)
    to_smem.start()
    to_smem.wait()

    for load in loads[4:]:
        load.wait()

    def fill(owner, into, at):
        first, second = table_s[0, owner] & 127, table_s[1, owner] & 127
        w0 = mask[first].astype(jnp.float32) * ivar[first].astype(jnp.float32)
        w1 = mask[second].astype(jnp.float32) * ivar[second].astype(jnp.float32)
        p0, p1 = w0 * pix[first], w1 * pix[second]
        into[pl.ds(at, 16), 0:PW] = jnp.concatenate([p0, p1], axis=0).astype(jnp.bfloat16)
        into[pl.ds(at, 16), PW : 2 * PW] = jnp.concatenate([w0, w1], axis=0).astype(jnp.bfloat16)

    def transfer(k, owner, group, target):
        rows = pl.ds(pl.multiple_of(k * 16, 16), 16)
        return (
            pltpu.make_async_remote_copy(
                src_ref=data.at[rows],
                dst_ref=data_in.at[rows],
                send_sem=data_send,
                recv_sem=data_recv.at[group],
                device_id=target,
                device_id_type=MESH,
            ),
            pltpu.make_async_remote_copy(
                src_ref=label.at[pl.ds(owner, 1)],
                dst_ref=label_in.at[pl.ds(k, 1)],
                send_sem=label_send,
                recv_sem=label_recv.at[group],
                device_id=target,
                device_id_type=MESH,
            ),
        )

    def send_some(first, last):
        group = first // 16
        words = [steps[group] for steps in (STEP_X, STEP_Y, STEP_Z, STEP_C)]

        def send(m, _):
            k = group * 16 + m
            dx, dy, dz, dc = [(jnp.int32(word) >> (2 * m)) & 3 for word in words]
            to_col = ((z + dz) & 3) * 2 + (core ^ dc)
            to_row = ((x + dx) & 3) * 4 + ((y + dy) & 3)
            owner = to_col * 16 + to_row
            fill(owner, data, pl.multiple_of(k * 16, 16))
            for copy in transfer(k, owner, group, (to_col, to_row)):
                copy.start()
            return 0

        lax.fori_loop(first - group * 16, last - group * 16, send, 0)

    pl.semaphore_wait(barrier, len(on_line))
    for peer in on_line:
        pl.semaphore_signal(line_sem, inc=1, device_id=peer, device_id_type=MESH)
    send_some(0, LINES)
    pl.semaphore_wait(line_sem, len(on_line))
    for peer in on_line[-3:]:
        pl.semaphore_signal(plane_sem, inc=1, device_id=peer, device_id_type=MESH)
    send_some(LINES, 16)
    for first in range(16, PLANES, 16):
        send_some(first, first + 16)
    pl.semaphore_wait(plane_sem, 3)
    for first in range(PLANES, 128, 16):
        send_some(first, min(first + 16, 127))
    fill(me, data_in, 127 * 16)
    own = pltpu.make_async_copy(label.at[pl.ds(me, 1)], label_in.at[pl.ds(127, 1)], table_sem)
    own.start()
    own.wait()

    taps_ref[...] = jnp.zeros_like(taps_ref)

    def build(b, _):
        combined = coef_ref[0, 0, 0, b] * basis_ref[0]
        for k in range(1, NBASIS):
            combined = combined + coef_ref[0, k, 0, b] * basis_ref[k]
        taps_ref[0:KS, 0:KS] = combined
        taps = taps_ref[...]
        for d in range(TAPS):
            i, s = d // GROUP, d % GROUP
            base = pltpu.roll(jnp.broadcast_to(taps[d : d + 1], (8, 128)), 0, 1, stride=1, stride_axis=0)
            spread = jnp.concatenate(
                [pltpu.roll(base, (128 - HALF + q) % 128, 1) for q in range(0, TILE, 8)], axis=0
            )
            weights[b, s * TILE : (s + 1) * TILE, i * 128 : (i + 1) * 128] = spread.astype(jnp.bfloat16)
        return 0

    lax.fori_loop(0, BANDS, build, 0)

    for group in range(8):
        count = 15 if group == 7 else 16
        big = pl.ds(group * 256, count * 16)
        small = pl.ds(group * 16, count)
        pltpu.make_async_remote_copy(
            src_ref=label.at[small], dst_ref=label_in.at[small], send_sem=label_send,
            recv_sem=label_recv.at[group], device_id=(col ^ 1, row), device_id_type=MESH,
        ).wait_recv()
        pltpu.make_async_remote_copy(
            src_ref=data.at[big], dst_ref=data_in.at[big], send_sem=data_send,
            recv_sem=data_recv.at[group], device_id=(col ^ 1, row), device_id_type=MESH,
        ).wait_recv()
        pick = iota((8, 128), 1) >> 4 == iota((8, 128), 0)
        lines = [
            jnp.sum(
                jnp.where(pick, label_in[group * 16 + h * 8 : group * 16 + h * 8 + 8].astype(jnp.float32), 0.0),
                axis=0,
                keepdims=True,
            )
            for h in range(2)
        ]
        line = jnp.concatenate(lines, axis=1).astype(jnp.int32)
        for b in range(BANDS):
            hit = iota((PH, 256), 0) + b * PH == line
            part = jnp.dot(
                hit.astype(jnp.float32).astype(jnp.bfloat16),
                data_in[group * 256 : (group + 1) * 256],
                preferred_element_type=jnp.float32,
            )
            if group:
                sums[b] += part
            else:
                sums[b] = part

    up, down = (row + 15) & 15, (row + 1) & 15
    left, right = (col + 7) & 7, (col + 1) & 7

    def halo(src, dst, i, target):
        return pltpu.make_async_remote_copy(
            src_ref=src, dst_ref=dst, send_sem=halo_send.at[i], recv_sem=halo_recv.at[i],
            device_id=target, device_id_type=MESH,
        )

    lane_p = iota((PH, 128), 1)
    pack_l = jnp.zeros((PH, 128), jnp.float32)
    pack_r = jnp.zeros((PH, 128), jnp.float32)
    for b in range(BANDS):
        mean = sums[b, :, 0:PW] / jnp.maximum(sums[b, :, PW : 2 * PW], 1.0)
        sums[b, :, 0:PW] = mean
        ends[0, b * HALF : (b + 1) * HALF] = mean[PH - HALF : PH]
        ends[1, b * HALF : (b + 1) * HALF] = mean[0:HALF]
        here = (lane_p >= b * HALF) & (lane_p < (b + 1) * HALF)
        pack_l = jnp.where(here, pltpu.roll(mean[:, 0:128], b * HALF, 1), pack_l)
        pack_r = jnp.where(here, pltpu.roll(mean[:, 128:256], (b * HALF + HALF) % 128, 1), pack_r)
    packs[0] = pack_l.astype(jnp.bfloat16)
    packs[1] = pack_r.astype(jnp.bfloat16)
    sides = [
        halo(packs.at[0], side_r.at[32 : 32 + PH], 2, (left, row)),
        halo(packs.at[1], side_l.at[32 : 32 + PH], 3, (right, row)),
    ]
    corners = [
        halo(packs.at[0, PH - 32 : PH], side_r.at[0:32], 4, (left, down)),
        halo(packs.at[1, PH - 32 : PH], side_l.at[0:32], 5, (right, down)),
        halo(packs.at[0, 0:32], side_r.at[32 + PH : ROWS], 6, (left, up)),
        halo(packs.at[1, 0:32], side_l.at[32 + PH : ROWS], 7, (right, up)),
    ]
    for copy in corners + sides:
        copy.start()
    ends[:, BANDS * HALF :] = jnp.zeros_like(ends[:, BANDS * HALF :])
    ends_b[...] = ends[...].astype(jnp.bfloat16)
    rows = [halo(ends_b.at[0], above, 0, (col, down)), halo(ends_b.at[1], below, 1, (col, up))]
    for copy in rows:
        copy.start()

    has_up, has_down, has_left, has_right = row > 0, row < 15, col > 0, col < 7

    def inner_windows(b, tile0, tile1, first):
        rows = tile0.shape[0]
        lanes = iota((rows, 128), 1)
        image32[b, pl.ds(4 * first + 1, rows, stride=4), :] = pltpu.roll(jnp.where(lanes < 32, tile1, tile0), 64, 1)
        image32[b, pl.ds(4 * first + 2, rows, stride=4), :] = jnp.where(lanes < 108, tile1, tile0)

    def outer_windows(b, tile0, tile1, edge_l, edge_r, first):
        rows = tile0.shape[0]
        lanes = iota((rows, 128), 1)
        edge_l = jnp.where(has_left, pltpu.roll(edge_l.astype(jnp.float32), (236 - b * HALF) % 128, 1), 0.0)
        edge_r = jnp.where(has_right, pltpu.roll(edge_r.astype(jnp.float32), (128 - b * HALF) % 128, 1), 0.0)
        image32[b, pl.ds(4 * first, rows, stride=4), :] = jnp.where(lanes < 108, tile0, edge_l)
        image32[b, pl.ds(4 * first + 3, rows, stride=4), :] = pltpu.roll(jnp.where(lanes < 32, edge_r, tile1), 64, 1)

    def widen(b, first, last, first2, last2):
        image2[b, first:last, 0:128] = image32[b, first:last].astype(jnp.bfloat16)
        image2[b, first2:last2, 128:256] = image32[b, first2 + 16 : last2 + 16].astype(jnp.bfloat16)

    def matmul(b, spans):
        pairs = [
            jnp.concatenate(
                [image2[b, 4 * FIRST + 32 * p + lo : 4 * FIRST + 32 * p + hi] for lo, hi in spans], axis=0
            )
            for p in range(SHIFTS // 2)
        ]
        if SHIFTS % 2:
            pairs.append(
                jnp.concatenate(
                    [
                        image2[b, 4 * FIRST + 16 * (SHIFTS - 1) + lo : 4 * FIRST + 16 * (SHIFTS - 1) + hi, 0:128]
                        for lo, hi in spans
                    ],
                    axis=0,
                )
            )
        result = lax.dot_general(
            jnp.concatenate(pairs, axis=1), weights[b], (((1,), (1,)), ((), ())), preferred_element_type=jnp.float32
        )
        at = 0
        for lo, hi in spans:
            full[b, lo:hi] = result[at : at + hi - lo]
            at += hi - lo

    def finish(b, lo, hi):
        first, last = 4 * lo, 4 * hi + 8
        prod[b, first:last] = full[b, first:last, 0:128] + full[b, first + 8 : last + 8, 128:256]
        rows = hi - lo
        lanes = iota((rows, 128), 1)
        for h in range(2):
            e0, e0n, e1, e1n = [prod[b, pl.ds(first + 2 * h + i, rows, stride=4), :] for i in (0, 4, 1, 5)]
            kept = jnp.where(lanes < TILE, e0, e1n)
            moved = jnp.where(lanes < TILE, e1, e0n)
            out_ref[b, lo:hi, h * 128 : (h + 1) * 128] = kept + pltpu.roll(moved, TILE, 1)

    for b in range(BANDS):
        inner_windows(b, sums[b, :, 0:128], sums[b, :, 128:256], 32)
        image32[b, LAST : LAST + 32] = jnp.zeros((32, 128), jnp.float32)
    for copy in sides:
        copy.wait_recv()
    for b in range(BANDS):
        outer_windows(
            b, sums[b, :, 0:128], sums[b, :, 128:256], side_l[32 : 32 + PH], side_r[32 : 32 + PH], 32
        )
        widen(b, 128, 640, 128, 608)
        matmul(b, ((80, 432),))
        finish(b, 24, 104)

    for copy in rows:
        copy.wait_recv()
    strips = ((0, 32 - HALF, 32 - HALF), (1, 0, 32 + PH))
    ends[0] = jnp.where(has_up, above[...].astype(jnp.float32), 0.0)
    ends[1] = jnp.where(has_down, below[...].astype(jnp.float32), 0.0)
    for b in range(BANDS):
        for i, _, first in strips:
            strip = ends[i, b * HALF : (b + 1) * HALF]
            inner_windows(b, strip[:, 0:128], strip[:, 128:256], first)
    for copy in corners:
        copy.wait_recv()
    for i, here, first in ((0, has_up, 0), (1, has_down, 32 + PH)):
        corner[i, 0] = jnp.where(here, side_l[first : first + 32].astype(jnp.float32), 0.0)
        corner[i, 1] = jnp.where(here, side_r[first : first + 32].astype(jnp.float32), 0.0)
    for b in range(BANDS):
        for i, at, first in strips:
            strip = ends[i, b * HALF : (b + 1) * HALF]
            outer_windows(
                b, strip[:, 0:128], strip[:, 128:256], corner[i, 0, at : at + HALF], corner[i, 1, at : at + HALF], first
            )
        widen(b, 48, 128, 48, 128)
        widen(b, 640, 736, 608, 736)
        matmul(b, ((0, 80), (432, OUT_ROWS)))
        finish(b, 0, 24)
        finish(b, 104, 128)

    for copy in sides + rows + corners:
        copy.wait_send()
    pltpu.make_async_remote_copy(
        src_ref=data.at[pl.ds(0, 127 * 16)], dst_ref=data_in.at[pl.ds(0, 127 * 16)], send_sem=data_send,
        recv_sem=data_recv.at[0], device_id=(col ^ 1, row), device_id_type=MESH,
    ).wait_send()
    pltpu.make_async_remote_copy(
        src_ref=label.at[pl.ds(0, 127)], dst_ref=label_in.at[pl.ds(0, 127)], send_sem=label_send,
        recv_sem=label_recv.at[0], device_id=(col ^ 1, row), device_id_type=MESH,
    ).wait_send()


def on_device(
    block_pixels,
    block_ivar,
    block_mask,
    block_patch,
    block_offset,
    block_exposure,
    exposure_band,
    basis,
    coefficients,
):
    f32, bf16, i32 = jnp.float32, jnp.bfloat16, jnp.int32
    lines = [v.reshape(1, v.size) for v in (block_patch, block_offset, block_exposure, exposure_band)]
    scales = coefficients.transpose(0, 3, 1, 2)
    vmem, smem, hbm = pltpu.VMEM, pltpu.SMEM, pltpu.HBM
    dma = pltpu.SemaphoreType.DMA
    return pl.pallas_call(
        body,
        out_shape=vmem((BANDS, PH, PW), f32),
        in_specs=[pl.BlockSpec(memory_space=hbm)] * 9,
        out_specs=pl.BlockSpec(memory_space=vmem),
        scratch_shapes=[
            vmem((128, BH, PW), f32),
            vmem((128, BH, PW), bf16),
            vmem((128, BH, PW), i32),
            vmem((1, 128), i32),
            vmem((1, 128), i32),
            vmem((1, 128), i32),
            vmem((1, exposure_band.size), i32),
            vmem(basis.shape, f32),
            smem(scales.shape, f32),
            vmem((TAPS, 128), f32),
            vmem((8, 128), i32),
            smem((8, 128), i32),
            vmem((128, 128), i32),
            vmem((128, 128), i32),
            vmem((2048, 2 * PW), bf16),
            vmem((2048, 2 * PW), bf16),
            vmem((BANDS, PH, 2 * PW), f32),
            vmem((BANDS, GROUP * TILE, SHIFTS * 128), bf16),
            vmem((2, 128, PW), f32),
            vmem((2, 128, PW), bf16),
            vmem((2, PH, 128), bf16),
            vmem((128, PW), bf16),
            vmem((128, PW), bf16),
            vmem((ROWS, 128), bf16),
            vmem((ROWS, 128), bf16),
            vmem((2, 2, 32, 128), f32),
            vmem((BANDS, 4 * ROWS + 8, 128), f32),
            vmem((BANDS, 4 * ROWS, 256), bf16),
            vmem((BANDS, OUT_ROWS, 256), f32),
            vmem((BANDS, OUT_ROWS, 128), f32),
            dma((9,)),
            dma,
            dma,
            dma((8,)),
            dma,
            dma((8,)),
            dma((8,)),
            dma((8,)),
            pltpu.SemaphoreType.REGULAR,
            pltpu.SemaphoreType.REGULAR,
        ],
        compiler_params=pltpu.CompilerParams(
            collective_id=0, has_side_effects=True, vmem_limit_bytes=56 << 20
        ),
        cost_estimate=pl.CostEstimate(flops=6 << 30, bytes_accessed=4 << 20, transcendentals=0),
    )(block_pixels, block_ivar, block_mask, *lines, basis, scales)


def solution(mesh):
    placed = (
        P(("col", "row"), None, None),
        P(("col", "row"), None, None),
        P(("col", "row"), None, None),
        P(("col", "row"), None),
        P(("col", "row")),
        P(("col", "row")),
        P(),
        P(),
        P("row", "col", None, None),
    )
    return jax.shard_map(
        on_device, mesh=mesh, in_specs=placed, out_specs=P(None, "row", "col"), check_vma=False
    )
```

```python
import jax
import jax.numpy as jnp
from jax import lax
from jax.experimental import pallas as pl
from jax.experimental.pallas import tpu as pltpu
from jax.sharding import PartitionSpec as P

BANDS = 6
NBASIS = 5
KS = 41
HALF = 20
PH = 128
PW = 256
BH = 8
MESH = pl.DeviceIdType.MESH

STEP_X = (537068576, 823337521, 1310237458, -246991694, -1782682714, -373949073, 1810198426, 930526717)
STEP_Y = (-2013216504, -1941156792, -1819924284, 1011993900, 1734851178, -1699252357, 1859770862, 904623991)
STEP_Z = (1758998594, 1031141806, 685869056, -853781559, 1524231834, -1497901570, -812206469, 14293)
STEP_C = (1431568384, 1431655765, 341, 0, 0, 1430257664, 1431655765, 357913941)
LINES, PLANES = 13, 64

GROUP = 4
TILE = 64
TAPS = 44
SHIFTS = TAPS // GROUP
ROWS = PH + 64
FIRST = 32 - HALF
OUT_ROWS = 528
LAST = 4 * (32 + PH + HALF)


def iota(shape, dim):
    return lax.broadcasted_iota(jnp.int32, shape, dim)


def body(
    pix_hbm,
    ivar_hbm,
    mask_hbm,
    patch_hbm,
    offset_hbm,
    exposure_hbm,
    band_hbm,
    basis_hbm,
    coef_hbm,
    out_ref,
    pix,
    ivar,
    mask,
    patch_ref,
    offset_ref,
    exposure_ref,
    band_ref,
    basis_ref,
    coef_ref,
    taps_ref,
    table,
    table_s,
    label,
    label_in,
    data,
    data_in,
    sums,
    weights,
    ends,
    ends_b,
    packs,
    above,
    below,
    side_l,
    side_r,
    corner,
    image32,
    image2,
    full,
    prod,
    in_sem,
    table_sem,
    data_send,
    data_recv,
    label_send,
    label_recv,
    halo_send,
    halo_recv,
    line_sem,
    plane_sem,
):
    col = lax.axis_index("col")
    row = lax.axis_index("row")
    me = col * 16 + row
    z, core, x, y = col >> 1, col & 1, row >> 2, row & 3

    loads = [
        pltpu.make_async_copy(src, dst, in_sem.at[i])
        for i, (src, dst) in enumerate(
            (
                (patch_hbm, patch_ref),
                (offset_hbm, offset_ref),
                (exposure_hbm, exposure_ref),
                (band_hbm, band_ref),
                (pix_hbm, pix),
                (ivar_hbm, ivar),
                (mask_hbm, mask),
                (basis_hbm, basis_ref),
                (coef_hbm, coef_ref),
            )
        )
    ]
    barrier = pltpu.get_barrier_semaphore()
    on_line = (
        [((col + d) & 7, row) for d in range(1, 8)]
        + [(col, x * 4 + ((y + d) & 3)) for d in range(1, 4)]
        + [(col, ((x + d) & 3) * 4 + y) for d in range(1, 4)]
    )
    for peer in on_line:
        pl.semaphore_signal(barrier, inc=1, device_id=peer, device_id_type=MESH)
    for load in loads:
        load.start()
    for load in loads[:4]:
        load.wait()

    square = (128, 128)
    sub, lane = iota(square, 0), iota(square, 1)
    diag = sub == lane

    def to_column(line):
        return jnp.sum(jnp.where(diag, line, 0.0), axis=1, keepdims=True)

    def to_line(column):
        return jnp.sum(jnp.where(diag, column, 0.0), axis=0, keepdims=True)

    subf, lanef = sub.astype(jnp.float32), lane.astype(jnp.float32)
    patch = patch_ref[...].astype(jnp.float32)
    exposures = band_ref.shape[1]
    band_line = jnp.broadcast_to(band_ref[...].astype(jnp.float32), (exposures, exposures))
    band_col = jnp.sum(
        jnp.where(iota(band_line.shape, 0) == iota(band_line.shape, 1), band_line, 0.0), axis=1, keepdims=True
    )
    band_line = jnp.sum(
        jnp.where(exposure_ref[...].astype(jnp.float32) == subf[0:exposures], band_col, 0.0), axis=0, keepdims=True
    )
    key_line = band_line * float(PH) + offset_ref[...].astype(jnp.float32)
    named = patch == subf
    low = jnp.min(jnp.where(named, lanef, 128.0), axis=1, keepdims=True)
    high = jnp.max(jnp.where(named, lanef, -1.0), axis=1, keepdims=True)
    key_low = jnp.sum(jnp.where(lanef == low, key_line, 0.0), axis=1, keepdims=True)
    key_high = jnp.sum(jnp.where(lanef == high, key_line, 0.0), axis=1, keepdims=True)
    key_low = jnp.where(low < 128.0, key_low, -1000.0)
    key_high = jnp.where(high > low, key_high, -1000.0)
    place = (lane & 15) < BH
    label[...] = (jnp.where(place, key_low, key_high) + (lane & 7).astype(jnp.float32)).astype(jnp.int32)
    low_line = to_line(jnp.minimum(low, 127.0))
    high_line = to_line(jnp.maximum(high, 0.0))
    table[...] = jnp.where(iota((8, 128), 0) == 0, low_line, high_line).astype(jnp.int32)
    to_smem = pltpu.make_async_copy(table, table_s, table_sem)
    to_smem.start()
    to_smem.wait()

    for load in loads[4:]:
        load.wait()

    def fill(owner, into, at):
        first, second = table_s[0, owner] & 127, table_s[1, owner] & 127
        w0 = mask[first].astype(jnp.float32) * ivar[first].astype(jnp.float32)
        w1 = mask[second].astype(jnp.float32) * ivar[second].astype(jnp.float32)
        p0, p1 = w0 * pix[first], w1 * pix[second]
        into[pl.ds(at, 16), 0:PW] = jnp.concatenate([p0, p1], axis=0).astype(jnp.bfloat16)
        into[pl.ds(at, 16), PW : 2 * PW] = jnp.concatenate([w0, w1], axis=0).astype(jnp.bfloat16)

    def transfer(k, owner, group, target):
        rows = pl.ds(pl.multiple_of(k * 16, 16), 16)
        return (
            pltpu.make_async_remote_copy(
                src_ref=data.at[rows],
                dst_ref=data_in.at[rows],
                send_sem=data_send,
                recv_sem=data_recv.at[group],
                device_id=target,
                device_id_type=MESH,
            ),
            pltpu.make_async_remote_copy(
                src_ref=label.at[pl.ds(owner, 1)],
                dst_ref=label_in.at[pl.ds(k, 1)],
                send_sem=label_send,
                recv_sem=label_recv.at[group],
                device_id=target,
                device_id_type=MESH,
            ),
        )

    def send_some(first, last):
        group = first // 16
        words = [steps[group] for steps in (STEP_X, STEP_Y, STEP_Z, STEP_C)]

        def send(m, _):
            k = group * 16 + m
            dx, dy, dz, dc = [(jnp.int32(word) >> (2 * m)) & 3 for word in words]
            to_col = ((z + dz) & 3) * 2 + (core ^ dc)
            to_row = ((x + dx) & 3) * 4 + ((y + dy) & 3)
            owner = to_col * 16 + to_row
            fill(owner, data, pl.multiple_of(k * 16, 16))
            for copy in transfer(k, owner, group, (to_col, to_row)):
                copy.start()
            return 0

        lax.fori_loop(first - group * 16, last - group * 16, send, 0)

    pl.semaphore_wait(barrier, len(on_line))
    for peer in on_line:
        pl.semaphore_signal(line_sem, inc=1, device_id=peer, device_id_type=MESH)
    send_some(0, LINES)
    pl.semaphore_wait(line_sem, len(on_line))
    for peer in on_line[-3:]:
        pl.semaphore_signal(plane_sem, inc=1, device_id=peer, device_id_type=MESH)
    send_some(LINES, 16)
    for first in range(16, PLANES, 16):
        send_some(first, first + 16)
    pl.semaphore_wait(plane_sem, 3)
    for first in range(PLANES, 128, 16):
        send_some(first, min(first + 16, 127))
    fill(me, data_in, 127 * 16)
    own = pltpu.make_async_copy(label.at[pl.ds(me, 1)], label_in.at[pl.ds(127, 1)], table_sem)
    own.start()
    own.wait()

    taps_ref[...] = jnp.zeros_like(taps_ref)

    def build(b, _):
        combined = coef_ref[0, 0, 0, b] * basis_ref[0]
        for k in range(1, NBASIS):
            combined = combined + coef_ref[0, k, 0, b] * basis_ref[k]
        taps_ref[0:KS, 0:KS] = combined
        taps = taps_ref[...]
        for d in range(TAPS):
            i, s = d // GROUP, d % GROUP
            base = pltpu.roll(jnp.broadcast_to(taps[d : d + 1], (8, 128)), 0, 1, stride=1, stride_axis=0)
            spread = jnp.concatenate(
                [pltpu.roll(base, (128 - HALF + q) % 128, 1) for q in range(0, TILE, 8)], axis=0
            )
            weights[b, s * TILE : (s + 1) * TILE, i * 128 : (i + 1) * 128] = spread.astype(jnp.bfloat16)
        return 0

    lax.fori_loop(0, BANDS, build, 0)

    for group in range(8):
        count = 15 if group == 7 else 16
        big = pl.ds(group * 256, count * 16)
        small = pl.ds(group * 16, count)
        pltpu.make_async_remote_copy(
            src_ref=label.at[small], dst_ref=label_in.at[small], send_sem=label_send,
            recv_sem=label_recv.at[group], device_id=(col ^ 1, row), device_id_type=MESH,
        ).wait_recv()
        pltpu.make_async_remote_copy(
            src_ref=data.at[big], dst_ref=data_in.at[big], send_sem=data_send,
            recv_sem=data_recv.at[group], device_id=(col ^ 1, row), device_id_type=MESH,
        ).wait_recv()
        pick = iota((8, 128), 1) >> 4 == iota((8, 128), 0)
        lines = [
            jnp.sum(
                jnp.where(pick, label_in[group * 16 + h * 8 : group * 16 + h * 8 + 8].astype(jnp.float32), 0.0),
                axis=0,
                keepdims=True,
            )
            for h in range(2)
        ]
        line = jnp.concatenate(lines, axis=1).astype(jnp.int32)
        for b in range(BANDS):
            hit = iota((PH, 256), 0) + b * PH == line
            part = jnp.dot(
                hit.astype(jnp.float32).astype(jnp.bfloat16),
                data_in[group * 256 : (group + 1) * 256],
                preferred_element_type=jnp.float32,
            )
            if group:
                sums[b] += part
            else:
                sums[b] = part

    up, down = (row + 15) & 15, (row + 1) & 15
    left, right = (col + 7) & 7, (col + 1) & 7

    def halo(src, dst, i, target):
        return pltpu.make_async_remote_copy(
            src_ref=src, dst_ref=dst, send_sem=halo_send.at[i], recv_sem=halo_recv.at[i],
            device_id=target, device_id_type=MESH,
        )

    has_up, has_down, has_left, has_right = row > 0, row < 15, col > 0, col < 7

    def start(copies):
        for copy, sends, _ in copies:
            pl.when(sends)(copy.start)

    def arrive(copies):
        for copy, _, receives in copies:
            pl.when(receives)(copy.wait_recv)

    def leave(copies):
        for copy, sends, _ in copies:
            pl.when(sends)(copy.wait_send)

    lane_p = iota((PH, 128), 1)
    pack_l = jnp.zeros((PH, 128), jnp.float32)
    pack_r = jnp.zeros((PH, 128), jnp.float32)
    for b in range(BANDS):
        mean = sums[b, :, 0:PW] / jnp.maximum(sums[b, :, PW : 2 * PW], 1.0)
        sums[b, :, 0:PW] = mean
        ends[0, b * HALF : (b + 1) * HALF] = mean[PH - HALF : PH]
        ends[1, b * HALF : (b + 1) * HALF] = mean[0:HALF]
        here = (lane_p >= b * HALF) & (lane_p < (b + 1) * HALF)
        pack_l = jnp.where(here, pltpu.roll(mean[:, 0:128], b * HALF, 1), pack_l)
        pack_r = jnp.where(here, pltpu.roll(mean[:, 128:256], (b * HALF + HALF) % 128, 1), pack_r)
    packs[0] = pack_l.astype(jnp.bfloat16)
    packs[1] = pack_r.astype(jnp.bfloat16)
    sides = [
        (halo(packs.at[0], side_r.at[32 : 32 + PH], 2, (left, row)), has_left, has_right),
        (halo(packs.at[1], side_l.at[32 : 32 + PH], 3, (right, row)), has_right, has_left),
    ]
    corners = [
        (
            halo(packs.at[0, PH - 32 : PH], side_r.at[0:32], 4, (left, down)),
            has_left & has_down,
            has_right & has_up,
        ),
        (
            halo(packs.at[1, PH - 32 : PH], side_l.at[0:32], 5, (right, down)),
            has_right & has_down,
            has_left & has_up,
        ),
        (
            halo(packs.at[0, 0:32], side_r.at[32 + PH : ROWS], 6, (left, up)),
            has_left & has_up,
            has_right & has_down,
        ),
        (
            halo(packs.at[1, 0:32], side_l.at[32 + PH : ROWS], 7, (right, up)),
            has_right & has_up,
            has_left & has_down,
        ),
    ]
    start(corners + sides)
    ends[:, BANDS * HALF :] = jnp.zeros_like(ends[:, BANDS * HALF :])
    ends_b[...] = ends[...].astype(jnp.bfloat16)
    rows = [
        (halo(ends_b.at[0], above, 0, (col, down)), has_down, has_up),
        (halo(ends_b.at[1], below, 1, (col, up)), has_up, has_down),
    ]
    start(rows)


    def inner_windows(b, tile0, tile1, first):
        rows = tile0.shape[0]
        lanes = iota((rows, 128), 1)
        image32[b, pl.ds(4 * first + 1, rows, stride=4), :] = pltpu.roll(jnp.where(lanes < 32, tile1, tile0), 64, 1)
        image32[b, pl.ds(4 * first + 2, rows, stride=4), :] = jnp.where(lanes < 108, tile1, tile0)

    def outer_windows(b, tile0, tile1, edge_l, edge_r, first):
        rows = tile0.shape[0]
        lanes = iota((rows, 128), 1)
        edge_l = jnp.where(has_left, pltpu.roll(edge_l.astype(jnp.float32), (236 - b * HALF) % 128, 1), 0.0)
        edge_r = jnp.where(has_right, pltpu.roll(edge_r.astype(jnp.float32), (128 - b * HALF) % 128, 1), 0.0)
        image32[b, pl.ds(4 * first, rows, stride=4), :] = jnp.where(lanes < 108, tile0, edge_l)
        image32[b, pl.ds(4 * first + 3, rows, stride=4), :] = pltpu.roll(jnp.where(lanes < 32, edge_r, tile1), 64, 1)

    def widen(b, first, last, first2, last2):
        image2[b, first:last, 0:128] = image32[b, first:last].astype(jnp.bfloat16)
        image2[b, first2:last2, 128:256] = image32[b, first2 + 16 : last2 + 16].astype(jnp.bfloat16)

    def matmul(b, spans):
        pairs = [
            jnp.concatenate(
                [image2[b, 4 * FIRST + 32 * p + lo : 4 * FIRST + 32 * p + hi] for lo, hi in spans], axis=0
            )
            for p in range(SHIFTS // 2)
        ]
        if SHIFTS % 2:
            pairs.append(
                jnp.concatenate(
                    [
                        image2[b, 4 * FIRST + 16 * (SHIFTS - 1) + lo : 4 * FIRST + 16 * (SHIFTS - 1) + hi, 0:128]
                        for lo, hi in spans
                    ],
                    axis=0,
                )
            )
        result = lax.dot_general(
            jnp.concatenate(pairs, axis=1), weights[b], (((1,), (1,)), ((), ())), preferred_element_type=jnp.float32
        )
        at = 0
        for lo, hi in spans:
            full[b, lo:hi] = result[at : at + hi - lo]
            at += hi - lo

    def finish(b, lo, hi):
        first, last = 4 * lo, 4 * hi + 8
        prod[b, first:last] = full[b, first:last, 0:128] + full[b, first + 8 : last + 8, 128:256]
        rows = hi - lo
        lanes = iota((rows, 128), 1)
        for h in range(2):
            e0, e0n, e1, e1n = [prod[b, pl.ds(first + 2 * h + i, rows, stride=4), :] for i in (0, 4, 1, 5)]
            kept = jnp.where(lanes < TILE, e0, e1n)
            moved = jnp.where(lanes < TILE, e1, e0n)
            out_ref[b, lo:hi, h * 128 : (h + 1) * 128] = kept + pltpu.roll(moved, TILE, 1)

    for b in range(BANDS):
        inner_windows(b, sums[b, :, 0:128], sums[b, :, 128:256], 32)
        image32[b, LAST : LAST + 32] = jnp.zeros((32, 128), jnp.float32)
    arrive(sides)
    for b in range(BANDS):
        outer_windows(
            b, sums[b, :, 0:128], sums[b, :, 128:256], side_l[32 : 32 + PH], side_r[32 : 32 + PH], 32
        )
        widen(b, 128, 640, 128, 608)
        matmul(b, ((80, 432),))
        finish(b, 24, 104)

    arrive(rows)
    strips = ((0, 32 - HALF, 32 - HALF), (1, 0, 32 + PH))
    ends[0] = jnp.where(has_up, above[...].astype(jnp.float32), 0.0)
    ends[1] = jnp.where(has_down, below[...].astype(jnp.float32), 0.0)
    for b in range(BANDS):
        for i, _, first in strips:
            strip = ends[i, b * HALF : (b + 1) * HALF]
            inner_windows(b, strip[:, 0:128], strip[:, 128:256], first)
    arrive(corners)
    for i, here, first in ((0, has_up, 0), (1, has_down, 32 + PH)):
        corner[i, 0] = jnp.where(here, side_l[first : first + 32].astype(jnp.float32), 0.0)
        corner[i, 1] = jnp.where(here, side_r[first : first + 32].astype(jnp.float32), 0.0)
    for b in range(BANDS):
        for i, at, first in strips:
            strip = ends[i, b * HALF : (b + 1) * HALF]
            outer_windows(
                b, strip[:, 0:128], strip[:, 128:256], corner[i, 0, at : at + HALF], corner[i, 1, at : at + HALF], first
            )
        widen(b, 48, 128, 48, 128)
        widen(b, 640, 736, 608, 736)
        matmul(b, ((0, 80), (432, OUT_ROWS)))
        finish(b, 0, 24)
        finish(b, 104, 128)

    leave(sides + rows + corners)
    pltpu.make_async_remote_copy(
        src_ref=data.at[pl.ds(0, 127 * 16)], dst_ref=data_in.at[pl.ds(0, 127 * 16)], send_sem=data_send,
        recv_sem=data_recv.at[0], device_id=(col ^ 1, row), device_id_type=MESH,
    ).wait_send()
    pltpu.make_async_remote_copy(
        src_ref=label.at[pl.ds(0, 127)], dst_ref=label_in.at[pl.ds(0, 127)], send_sem=label_send,
        recv_sem=label_recv.at[0], device_id=(col ^ 1, row), device_id_type=MESH,
    ).wait_send()


def on_device(
    block_pixels,
    block_ivar,
    block_mask,
    block_patch,
    block_offset,
    block_exposure,
    exposure_band,
    basis,
    coefficients,
):
    f32, bf16, i32 = jnp.float32, jnp.bfloat16, jnp.int32
    lines = [v.reshape(1, v.size) for v in (block_patch, block_offset, block_exposure, exposure_band)]
    scales = coefficients.transpose(0, 3, 1, 2)
    vmem, smem, hbm = pltpu.VMEM, pltpu.SMEM, pltpu.HBM
    dma = pltpu.SemaphoreType.DMA
    return pl.pallas_call(
        body,
        out_shape=vmem((BANDS, PH, PW), f32),
        in_specs=[pl.BlockSpec(memory_space=hbm)] * 9,
        out_specs=pl.BlockSpec(memory_space=vmem),
        scratch_shapes=[
            vmem((128, BH, PW), f32),
            vmem((128, BH, PW), bf16),
            vmem((128, BH, PW), i32),
            vmem((1, 128), i32),
            vmem((1, 128), i32),
            vmem((1, 128), i32),
            vmem((1, exposure_band.size), i32),
            vmem(basis.shape, f32),
            smem(scales.shape, f32),
            vmem((TAPS, 128), f32),
            vmem((8, 128), i32),
            smem((8, 128), i32),
            vmem((128, 128), i32),
            vmem((128, 128), i32),
            vmem((2048, 2 * PW), bf16),
            vmem((2048, 2 * PW), bf16),
            vmem((BANDS, PH, 2 * PW), f32),
            vmem((BANDS, GROUP * TILE, SHIFTS * 128), bf16),
            vmem((2, 128, PW), f32),
            vmem((2, 128, PW), bf16),
            vmem((2, PH, 128), bf16),
            vmem((128, PW), bf16),
            vmem((128, PW), bf16),
            vmem((ROWS, 128), bf16),
            vmem((ROWS, 128), bf16),
            vmem((2, 2, 32, 128), f32),
            vmem((BANDS, 4 * ROWS + 8, 128), f32),
            vmem((BANDS, 4 * ROWS, 256), bf16),
            vmem((BANDS, OUT_ROWS, 256), f32),
            vmem((BANDS, OUT_ROWS, 128), f32),
            dma((9,)),
            dma,
            dma,
            dma((8,)),
            dma,
            dma((8,)),
            dma((8,)),
            dma((8,)),
            pltpu.SemaphoreType.REGULAR,
            pltpu.SemaphoreType.REGULAR,
        ],
        compiler_params=pltpu.CompilerParams(
            collective_id=0, has_side_effects=True, vmem_limit_bytes=56 << 20
        ),
        cost_estimate=pl.CostEstimate(flops=6 << 30, bytes_accessed=4 << 20, transcendentals=0),
    )(block_pixels, block_ivar, block_mask, *lines, basis, scales)


def solution(mesh):
    placed = (
        P(("col", "row"), None, None),
        P(("col", "row"), None, None),
        P(("col", "row"), None, None),
        P(("col", "row"), None),
        P(("col", "row")),
        P(("col", "row")),
        P(),
        P(),
        P("row", "col", None, None),
    )
    return jax.shard_map(
        on_device, mesh=mesh, in_specs=placed, out_specs=P(None, "row", "col"), check_vma=False
    )
```

```python
import jax
import jax.numpy as jnp
from jax import lax
from jax.experimental import pallas as pl
from jax.experimental.pallas import tpu as pltpu
from jax.sharding import PartitionSpec as P

BANDS = 6
NBASIS = 5
KS = 41
HALF = 20
PH = 128
PW = 256
BH = 8
MESH = pl.DeviceIdType.MESH

STEP_X = (537068576, 823337521, 1310237458, -246991694, -1782682714, -373949073, 1810198426, 930526717)
STEP_Y = (-2013216504, -1941156792, -1819924284, 1011993900, 1734851178, -1699252357, 1859770862, 904623991)
STEP_Z = (1758998594, 1031141806, 685869056, -853781559, 1524231834, -1497901570, -812206469, 14293)
STEP_C = (1431568384, 1431655765, 341, 0, 0, 1430257664, 1431655765, 357913941)
LINES, PLANES = 13, 64

GROUP = 4
TILE = 64
TAPS = 44
SHIFTS = TAPS // GROUP
ROWS = PH + 64
FIRST = 32 - HALF
OUT_ROWS = 528
LAST = 4 * (32 + PH + HALF)


def iota(shape, dim):
    return lax.broadcasted_iota(jnp.int32, shape, dim)


def body(
    pix_hbm,
    ivar_hbm,
    mask_hbm,
    patch_hbm,
    offset_hbm,
    exposure_hbm,
    band_hbm,
    basis_hbm,
    coef_hbm,
    out_ref,
    pix,
    ivar,
    mask,
    patch_ref,
    offset_ref,
    exposure_ref,
    band_ref,
    basis_ref,
    coef_ref,
    taps_ref,
    table,
    table_s,
    label,
    label_in,
    data,
    data_in,
    sums,
    weights,
    ends,
    ends_b,
    packs,
    above,
    below,
    side_l,
    side_r,
    corner,
    image32,
    image2,
    full,
    prod,
    in_sem,
    table_sem,
    data_send,
    data_recv,
    label_send,
    label_recv,
    halo_send,
    halo_recv,
    line_sem,
    plane_sem,
):
    col = lax.axis_index("col")
    row = lax.axis_index("row")
    me = col * 16 + row
    z, core, x, y = col >> 1, col & 1, row >> 2, row & 3

    loads = [
        pltpu.make_async_copy(src, dst, in_sem.at[i])
        for i, (src, dst) in enumerate(
            (
                (patch_hbm, patch_ref),
                (offset_hbm, offset_ref),
                (exposure_hbm, exposure_ref),
                (band_hbm, band_ref),
                (pix_hbm, pix),
                (ivar_hbm, ivar),
                (mask_hbm, mask),
                (basis_hbm, basis_ref),
                (coef_hbm, coef_ref),
            )
        )
    ]
    barrier = pltpu.get_barrier_semaphore()
    on_line = (
        [((col + d) & 7, row) for d in range(1, 8)]
        + [(col, x * 4 + ((y + d) & 3)) for d in range(1, 4)]
        + [(col, ((x + d) & 3) * 4 + y) for d in range(1, 4)]
    )
    for peer in on_line:
        pl.semaphore_signal(barrier, inc=1, device_id=peer, device_id_type=MESH)
    for load in loads:
        load.start()
    for load in loads[:4]:
        load.wait()

    square = (128, 128)
    sub, lane = iota(square, 0), iota(square, 1)
    diag = sub == lane

    def to_column(line):
        return jnp.sum(jnp.where(diag, line, 0.0), axis=1, keepdims=True)

    def to_line(column):
        return jnp.sum(jnp.where(diag, column, 0.0), axis=0, keepdims=True)

    subf, lanef = sub.astype(jnp.float32), lane.astype(jnp.float32)
    patch = patch_ref[...].astype(jnp.float32)
    exposures = band_ref.shape[1]
    band_line = jnp.broadcast_to(band_ref[...].astype(jnp.float32), (exposures, exposures))
    band_col = jnp.sum(
        jnp.where(iota(band_line.shape, 0) == iota(band_line.shape, 1), band_line, 0.0), axis=1, keepdims=True
    )
    band_line = jnp.sum(
        jnp.where(exposure_ref[...].astype(jnp.float32) == subf[0:exposures], band_col, 0.0), axis=0, keepdims=True
    )
    key_line = band_line * float(PH) + offset_ref[...].astype(jnp.float32)
    named = patch == subf
    low = jnp.min(jnp.where(named, lanef, 128.0), axis=1, keepdims=True)
    high = jnp.max(jnp.where(named, lanef, -1.0), axis=1, keepdims=True)
    key_low = jnp.sum(jnp.where(lanef == low, key_line, 0.0), axis=1, keepdims=True)
    key_high = jnp.sum(jnp.where(lanef == high, key_line, 0.0), axis=1, keepdims=True)
    key_low = jnp.where(low < 128.0, key_low, -1000.0)
    key_high = jnp.where(high > low, key_high, -1000.0)
    place = (lane & 15) < BH
    label[...] = (jnp.where(place, key_low, key_high) + (lane & 7).astype(jnp.float32)).astype(jnp.int32)
    low_line = to_line(jnp.minimum(low, 127.0))
    high_line = to_line(jnp.maximum(high, 0.0))
    table[...] = jnp.where(iota((8, 128), 0) == 0, low_line, high_line).astype(jnp.int32)
    to_smem = pltpu.make_async_copy(table, table_s, table_sem)
    to_smem.start()
    to_smem.wait()

    for load in loads[4:]:
        load.wait()

    def fill(owner, into, at):
        first, second = table_s[0, owner] & 127, table_s[1, owner] & 127
        w0 = mask[first].astype(jnp.float32) * ivar[first].astype(jnp.float32)
        w1 = mask[second].astype(jnp.float32) * ivar[second].astype(jnp.float32)
        p0, p1 = w0 * pix[first], w1 * pix[second]
        into[pl.ds(at, 16), 0:PW] = jnp.concatenate([p0, p1], axis=0).astype(jnp.bfloat16)
        into[pl.ds(at, 16), PW : 2 * PW] = jnp.concatenate([w0, w1], axis=0).astype(jnp.bfloat16)

    def transfer(k, owner, group, target):
        rows = pl.ds(pl.multiple_of(k * 16, 16), 16)
        return (
            pltpu.make_async_remote_copy(
                src_ref=data.at[rows],
                dst_ref=data_in.at[rows],
                send_sem=data_send,
                recv_sem=data_recv.at[group],
                device_id=target,
                device_id_type=MESH,
            ),
            pltpu.make_async_remote_copy(
                src_ref=label.at[pl.ds(owner, 1)],
                dst_ref=label_in.at[pl.ds(k, 1)],
                send_sem=label_send,
                recv_sem=label_recv.at[group],
                device_id=target,
                device_id_type=MESH,
            ),
        )

    def send_some(first, last):
        group = first // 16
        words = [steps[group] for steps in (STEP_X, STEP_Y, STEP_Z, STEP_C)]

        def send(m, _):
            k = group * 16 + m
            dx, dy, dz, dc = [(jnp.int32(word) >> (2 * m)) & 3 for word in words]
            to_col = ((z + dz) & 3) * 2 + (core ^ dc)
            to_row = ((x + dx) & 3) * 4 + ((y + dy) & 3)
            owner = to_col * 16 + to_row
            fill(owner, data, pl.multiple_of(k * 16, 16))
            for copy in transfer(k, owner, group, (to_col, to_row)):
                copy.start()
            return 0

        lax.fori_loop(first - group * 16, last - group * 16, send, 0)

    pl.semaphore_wait(barrier, len(on_line))
    for peer in on_line:
        pl.semaphore_signal(line_sem, inc=1, device_id=peer, device_id_type=MESH)
    send_some(0, LINES)
    pl.semaphore_wait(line_sem, len(on_line))
    for peer in on_line[-3:]:
        pl.semaphore_signal(plane_sem, inc=1, device_id=peer, device_id_type=MESH)
    send_some(LINES, 16)
    for first in range(16, PLANES, 16):
        send_some(first, first + 16)
    pl.semaphore_wait(plane_sem, 3)
    for first in range(PLANES, 128, 16):
        send_some(first, min(first + 16, 127))
    fill(me, data_in, 127 * 16)
    own = pltpu.make_async_copy(label.at[pl.ds(me, 1)], label_in.at[pl.ds(127, 1)], table_sem)
    own.start()
    own.wait()

    taps_ref[...] = jnp.zeros_like(taps_ref)

    def build(b, _):
        combined = coef_ref[0, 0, 0, b] * basis_ref[0]
        for k in range(1, NBASIS):
            combined = combined + coef_ref[0, k, 0, b] * basis_ref[k]
        taps_ref[0:KS, 0:KS] = combined
        taps = taps_ref[...]
        for d in range(TAPS):
            i, s = d // GROUP, d % GROUP
            base = pltpu.roll(jnp.broadcast_to(taps[d : d + 1], (8, 128)), 0, 1, stride=1, stride_axis=0)
            spread = jnp.concatenate(
                [pltpu.roll(base, (128 - HALF + q) % 128, 1) for q in range(0, TILE, 8)], axis=0
            )
            weights[b, s * TILE : (s + 1) * TILE, i * 128 : (i + 1) * 128] = spread.astype(jnp.bfloat16)
        return 0

    lax.fori_loop(0, BANDS, build, 0)

    for group in range(8):
        count = 15 if group == 7 else 16
        big = pl.ds(group * 256, count * 16)
        small = pl.ds(group * 16, count)
        pltpu.make_async_remote_copy(
            src_ref=label.at[small], dst_ref=label_in.at[small], send_sem=label_send,
            recv_sem=label_recv.at[group], device_id=(col ^ 1, row), device_id_type=MESH,
        ).wait_recv()
        pltpu.make_async_remote_copy(
            src_ref=data.at[big], dst_ref=data_in.at[big], send_sem=data_send,
            recv_sem=data_recv.at[group], device_id=(col ^ 1, row), device_id_type=MESH,
        ).wait_recv()
        pick = iota((8, 128), 1) >> 4 == iota((8, 128), 0)
        lines = [
            jnp.sum(
                jnp.where(pick, label_in[group * 16 + h * 8 : group * 16 + h * 8 + 8].astype(jnp.float32), 0.0),
                axis=0,
                keepdims=True,
            )
            for h in range(2)
        ]
        line = jnp.concatenate(lines, axis=1).astype(jnp.int32)
        for b in range(BANDS):
            hit = iota((PH, 256), 0) + b * PH == line
            part = jnp.dot(
                hit.astype(jnp.float32).astype(jnp.bfloat16),
                data_in[group * 256 : (group + 1) * 256],
                preferred_element_type=jnp.float32,
            )
            if group:
                sums[b] += part
            else:
                sums[b] = part

    up, down = (row + 15) & 15, (row + 1) & 15
    left, right = (col + 7) & 7, (col + 1) & 7

    def halo(src, dst, i, target):
        return pltpu.make_async_remote_copy(
            src_ref=src, dst_ref=dst, send_sem=halo_send.at[i], recv_sem=halo_recv.at[i],
            device_id=target, device_id_type=MESH,
        )

    has_up, has_down, has_left, has_right = row > 0, row < 15, col > 0, col < 7

    def start(copies):
        for copy, sends, _ in copies:
            pl.when(sends)(copy.start)

    def arrive(copies):
        for copy, _, receives in copies:
            pl.when(receives)(copy.wait_recv)

    def leave(copies):
        for copy, sends, _ in copies:
            pl.when(sends)(copy.wait_send)

    lane_p = iota((PH, 128), 1)
    pack_l = jnp.zeros((PH, 128), jnp.float32)
    pack_r = jnp.zeros((PH, 128), jnp.float32)
    for b in range(BANDS):
        mean = sums[b, :, 0:PW] / jnp.maximum(sums[b, :, PW : 2 * PW], 1.0)
        sums[b, :, 0:PW] = mean
        ends[0, b * HALF : (b + 1) * HALF] = mean[PH - HALF : PH]
        ends[1, b * HALF : (b + 1) * HALF] = mean[0:HALF]
        here = (lane_p >= b * HALF) & (lane_p < (b + 1) * HALF)
        pack_l = jnp.where(here, pltpu.roll(mean[:, 0:128], b * HALF, 1), pack_l)
        pack_r = jnp.where(here, pltpu.roll(mean[:, 128:256], (b * HALF + HALF) % 128, 1), pack_r)
    packs[0] = pack_l.astype(jnp.bfloat16)
    packs[1] = pack_r.astype(jnp.bfloat16)
    sides = [
        (halo(packs.at[0], side_r.at[32 : 32 + PH], 2, (left, row)), has_left, has_right),
        (halo(packs.at[1], side_l.at[32 : 32 + PH], 3, (right, row)), has_right, has_left),
    ]
    corners = [
        (
            halo(packs.at[0, PH - 32 : PH], side_r.at[0:32], 4, (left, down)),
            has_left & has_down,
            has_right & has_up,
        ),
        (
            halo(packs.at[1, PH - 32 : PH], side_l.at[0:32], 5, (right, down)),
            has_right & has_down,
            has_left & has_up,
        ),
        (
            halo(packs.at[0, 0:32], side_r.at[32 + PH : ROWS], 6, (left, up)),
            has_left & has_up,
            has_right & has_down,
        ),
        (
            halo(packs.at[1, 0:32], side_l.at[32 + PH : ROWS], 7, (right, up)),
            has_right & has_up,
            has_left & has_down,
        ),
    ]
    start(corners + sides)
    ends[:, BANDS * HALF :] = jnp.zeros_like(ends[:, BANDS * HALF :])
    ends_b[...] = ends[...].astype(jnp.bfloat16)
    rows = [
        (halo(ends_b.at[0], above, 0, (col, down)), has_down, has_up),
        (halo(ends_b.at[1], below, 1, (col, up)), has_up, has_down),
    ]
    start(rows)


    def inner_windows(b, tile0, tile1, first):
        rows = tile0.shape[0]
        lanes = iota((rows, 128), 1)
        image32[b, pl.ds(4 * first + 1, rows, stride=4), :] = pltpu.roll(jnp.where(lanes < 32, tile1, tile0), 64, 1)
        image32[b, pl.ds(4 * first + 2, rows, stride=4), :] = jnp.where(lanes < 108, tile1, tile0)

    def outer_windows(b, tile0, tile1, edge_l, edge_r, first):
        rows = tile0.shape[0]
        lanes = iota((rows, 128), 1)
        edge_l = jnp.where(has_left, pltpu.roll(edge_l.astype(jnp.float32), (236 - b * HALF) % 128, 1), 0.0)
        edge_r = jnp.where(has_right, pltpu.roll(edge_r.astype(jnp.float32), (128 - b * HALF) % 128, 1), 0.0)
        image32[b, pl.ds(4 * first, rows, stride=4), :] = jnp.where(lanes < 108, tile0, edge_l)
        image32[b, pl.ds(4 * first + 3, rows, stride=4), :] = pltpu.roll(jnp.where(lanes < 32, edge_r, tile1), 64, 1)

    def widen(b, first, last, first2, last2):
        image2[b, first:last, 0:128] = image32[b, first:last].astype(jnp.bfloat16)
        image2[b, first2:last2, 128:256] = image32[b, first2 + 16 : last2 + 16].astype(jnp.bfloat16)

    def matmul(b, spans):
        pairs = [
            jnp.concatenate(
                [image2[b, 4 * FIRST + 32 * p + lo : 4 * FIRST + 32 * p + hi] for lo, hi in spans], axis=0
            )
            for p in range(SHIFTS // 2)
        ]
        if SHIFTS % 2:
            pairs.append(
                jnp.concatenate(
                    [
                        image2[b, 4 * FIRST + 16 * (SHIFTS - 1) + lo : 4 * FIRST + 16 * (SHIFTS - 1) + hi, 0:128]
                        for lo, hi in spans
                    ],
                    axis=0,
                )
            )
        result = lax.dot_general(
            jnp.concatenate(pairs, axis=1), weights[b], (((1,), (1,)), ((), ())), preferred_element_type=jnp.float32
        )
        at = 0
        for lo, hi in spans:
            full[b, lo:hi] = result[at : at + hi - lo]
            at += hi - lo

    def finish(b, lo, hi):
        first, last = 4 * lo, 4 * hi + 8
        prod[b, first:last] = full[b, first:last, 0:128] + full[b, first + 8 : last + 8, 128:256]
        rows = hi - lo
        lanes = iota((rows, 128), 1)
        for h in range(2):
            e0, e0n, e1, e1n = [prod[b, pl.ds(first + 2 * h + i, rows, stride=4), :] for i in (0, 4, 1, 5)]
            kept = jnp.where(lanes < TILE, e0, e1n)
            moved = jnp.where(lanes < TILE, e1, e0n)
            out_ref[b, lo:hi, h * 128 : (h + 1) * 128] = kept + pltpu.roll(moved, TILE, 1)

    for b in range(BANDS):
        inner_windows(b, sums[b, :, 0:128], sums[b, :, 128:256], 32)
        image32[b, LAST : LAST + 32] = jnp.zeros((32, 128), jnp.float32)
    arrive(sides)
    for b in range(BANDS):
        outer_windows(
            b, sums[b, :, 0:128], sums[b, :, 128:256], side_l[32 : 32 + PH], side_r[32 : 32 + PH], 32
        )
        widen(b, 128, 640, 128, 608)
        matmul(b, ((80, 432),))
        finish(b, 24, 104)

    arrive(rows)
    strips = ((0, 32 - HALF, 32 - HALF), (1, 0, 32 + PH))
    ends[0] = jnp.where(has_up, above[...].astype(jnp.float32), 0.0)
    ends[1] = jnp.where(has_down, below[...].astype(jnp.float32), 0.0)
    for b in range(BANDS):
        for i, _, first in strips:
            strip = ends[i, b * HALF : (b + 1) * HALF]
            inner_windows(b, strip[:, 0:128], strip[:, 128:256], first)
    arrive(corners)
    for i, here, first in ((0, has_up, 0), (1, has_down, 32 + PH)):
        corner[i, 0, 0:32] = jnp.where(here, side_l[first : first + 32].astype(jnp.float32), 0.0)
        corner[i, 1, 0:32] = jnp.where(here, side_r[first : first + 32].astype(jnp.float32), 0.0)
    for b in range(BANDS):
        for i, at, first in strips:
            strip = ends[i, b * HALF : (b + 1) * HALF]
            outer_windows(
                b, strip[:, 0:128], strip[:, 128:256], corner[i, 0, at : at + HALF], corner[i, 1, at : at + HALF], first
            )
        widen(b, 48, 128, 48, 128)
        widen(b, 640, 736, 608, 736)
        matmul(b, ((0, 80), (432, OUT_ROWS)))
        finish(b, 0, 24)
        finish(b, 104, 128)

    leave(sides + rows + corners)
    pltpu.make_async_remote_copy(
        src_ref=data.at[pl.ds(0, 127 * 16)], dst_ref=data_in.at[pl.ds(0, 127 * 16)], send_sem=data_send,
        recv_sem=data_recv.at[0], device_id=(col ^ 1, row), device_id_type=MESH,
    ).wait_send()
    pltpu.make_async_remote_copy(
        src_ref=label.at[pl.ds(0, 127)], dst_ref=label_in.at[pl.ds(0, 127)], send_sem=label_send,
        recv_sem=label_recv.at[0], device_id=(col ^ 1, row), device_id_type=MESH,
    ).wait_send()


def on_device(
    block_pixels,
    block_ivar,
    block_mask,
    block_patch,
    block_offset,
    block_exposure,
    exposure_band,
    basis,
    coefficients,
):
    f32, bf16, i32 = jnp.float32, jnp.bfloat16, jnp.int32
    lines = [v.reshape(1, v.size) for v in (block_patch, block_offset, block_exposure, exposure_band)]
    scales = coefficients.transpose(0, 3, 1, 2)
    vmem, smem, hbm = pltpu.VMEM, pltpu.SMEM, pltpu.HBM
    dma = pltpu.SemaphoreType.DMA
    return pl.pallas_call(
        body,
        out_shape=vmem((BANDS, PH, PW), f32),
        in_specs=[pl.BlockSpec(memory_space=hbm)] * 9,
        out_specs=pl.BlockSpec(memory_space=vmem),
        scratch_shapes=[
            vmem((128, BH, PW), f32),
            vmem((128, BH, PW), bf16),
            vmem((128, BH, PW), i32),
            vmem((1, 128), i32),
            vmem((1, 128), i32),
            vmem((1, 128), i32),
            vmem((1, exposure_band.size), i32),
            vmem(basis.shape, f32),
            smem(scales.shape, f32),
            vmem((TAPS + 4, 128), f32),
            vmem((8, 128), i32),
            smem((8, 128), i32),
            vmem((128, 128), i32),
            vmem((128, 128), i32),
            vmem((2048, 2 * PW), bf16),
            vmem((2048, 2 * PW), bf16),
            vmem((BANDS, PH, 2 * PW), f32),
            vmem((BANDS, GROUP * TILE, SHIFTS * 128), bf16),
            vmem((2, 128, PW), f32),
            vmem((2, 128, PW), bf16),
            vmem((2, PH, 128), bf16),
            vmem((128, PW), bf16),
            vmem((128, PW), bf16),
            vmem((ROWS, 128), bf16),
            vmem((ROWS, 128), bf16),
            vmem((2, 2, 48, 128), f32),
            vmem((BANDS, 4 * ROWS + 8, 128), f32),
            vmem((BANDS, 4 * ROWS, 256), bf16),
            vmem((BANDS, OUT_ROWS, 256), f32),
            vmem((BANDS, OUT_ROWS, 128), f32),
            dma((9,)),
            dma,
            dma,
            dma((8,)),
            dma,
            dma((8,)),
            dma((8,)),
            dma((8,)),
            pltpu.SemaphoreType.REGULAR,
            pltpu.SemaphoreType.REGULAR,
        ],
        compiler_params=pltpu.CompilerParams(
            collective_id=0, has_side_effects=True, vmem_limit_bytes=56 << 20
        ),
        cost_estimate=pl.CostEstimate(flops=6 << 30, bytes_accessed=4 << 20, transcendentals=0),
    )(block_pixels, block_ivar, block_mask, *lines, basis, scales)


def solution(mesh):
    placed = (
        P(("col", "row"), None, None),
        P(("col", "row"), None, None),
        P(("col", "row"), None, None),
        P(("col", "row"), None),
        P(("col", "row")),
        P(("col", "row")),
        P(),
        P(),
        P("row", "col", None, None),
    )
    return jax.shard_map(
        on_device, mesh=mesh, in_specs=placed, out_specs=P(None, "row", "col"), check_vma=False
    )
```
